256 devices in a mesh: rows: 32 (over y, z), cols: 8 (over x, core).
Axes of the slice: x: 4, y: 4, z: 8, core: 2. Of those that a mesh axis runs over, the one named last changes fastest.
Arguments:
- samples: float32 [128, 131072], P('cols', 'rows')
- loadings: bfloat16 [256, 131072], P(None, 'rows')
- omega_tiles: float32 [1280, 512, 512], P(('rows', 'cols')), may hold values from -0.18 to 0.18
- omega_diagonal: float32 [131072], P('rows'), may hold values from 0.5 to 2
- tile_rows: int32 [1280], replicated, may hold values from 0 to 255, as said below
- tile_cols: int32 [1280], replicated, may hold values from 0 to 255, as said below
Outputs:
- new_tiles: float32 [1280, 512, 512], P(('rows', 'cols'))
- new_diagonal: float32 [131072], P('rows')
The draws below stay inside these ranges and needn't reach their ends.
Inputs may be any that keep to these rules, and one draw needn't show every extreme that they name: Slot s belongs to group g = s // 40; tile_rows[s] lies between g * 8 and g * 8 + 7. A block row may hold any number of tiles, none included. `tile_cols`: of the 40 tiles of one group, at most 3 have column blocks in any one group h (blocks h * 8 to h * 8 + 7), and in every group exactly 3 have column blocks in some one group.
All inputs are finite; a program needn't handle non-finite values.
Results may differ from the reference program's by a relative error of at most 0.0003.
Values sent between devices are 32-bit elements; how exact they have to be, the bound alone decides.
A program may use at most 64 MiB of HBM per device.

```python
import math
import jax
import jax.numpy as jnp
from jax import lax

BS = 512
K = 256
BR_DEV = 8
P_SIZE = 131072
NS = 128
GROUP_TILES = 40
CAP = 3
TILES = 1280
N_ROWS = 32


def factor_parts(key):
    base_key = jax.random.fold_in(key, 4242)
    key_load, key_score, key_noise = jax.random.split(base_key, 3)
    factor_load = (jax.random.normal(key_load, (K, P_SIZE), jnp.float32) * P_SIZE ** (-0.5)).astype(jnp.bfloat16)
    latent = jax.random.normal(key_score, (NS, K), jnp.float32) * (P_SIZE / K) ** 0.5
    noise = jax.random.normal(key_noise, (NS, P_SIZE), jnp.float32)
    data = jnp.dot(latent, factor_load.astype(jnp.float32), precision=lax.Precision.HIGHEST) + noise
    return (factor_load, data)


def draw_samples(key, part):
    return factor_parts(key)[1]


def draw_loadings(key, part):
    return factor_parts(key)[0]


def pattern(key):
    base_key = jax.random.fold_in(key, 777)

    def draw_group(group):
        group_key = jax.random.fold_in(base_key, group)
        key_rows, key_hot, key_order, key_shuffle, key_cols = jax.random.split(group_key, 5)
        local_rows = jax.random.randint(key_rows, (GROUP_TILES,), 0, BR_DEV)
        slot_group = jnp.arange(N_ROWS * CAP) // CAP
        within = jnp.arange(N_ROWS * CAP) % CAP
        hot_group = jax.random.randint(key_hot, (), 0, N_ROWS)
        order_keys = jax.random.permutation(key_order, N_ROWS * CAP) + CAP
        order_keys = jnp.where(slot_group == hot_group, within, order_keys)
        picked = slot_group[jnp.argsort(order_keys)[:GROUP_TILES]]
        shuffle = jax.random.permutation(key_shuffle, GROUP_TILES)
        groups = picked[shuffle]
        local_cols = jax.random.randint(key_cols, (GROUP_TILES,), 0, BR_DEV)
        return (group * BR_DEV + local_rows, groups * BR_DEV + local_cols)
    row_ids, col_ids = jax.vmap(draw_group)(jnp.arange(N_ROWS))
    return (row_ids.reshape(-1).astype(jnp.int32), col_ids.reshape(-1).astype(jnp.int32))


def draw_tile_rows(key, part):
    return pattern(key)[0]


def draw_tile_cols(key, part):
    return pattern(key)[1]


def block_levels(key, shape, shards, low, largest):
    def one(axis_at, parts):
        draws = jax.random.uniform(jax.random.fold_in(jax.random.fold_in(key, 6), axis_at), (parts,), jnp.float32, low / len(shards), largest / len(shards))
        return jnp.repeat(jnp.exp(draws), shape[axis_at] // parts).reshape((-1,) + (1,) * (len(shape) - axis_at - 1))

    factor_of = one(*shards[0])
    for cut in shards[1:]:
        factor_of = factor_of * one(*cut)
    return factor_of


def gaussian(key, dims, scale, reach, cuts=(), kind=jnp.bfloat16):
    entries = jax.random.normal(key, dims, jnp.float32) * scale
    if len(cuts) > 0:
        entries = block_levels(key, dims, cuts, -0.22, 0.18) * entries
    return jnp.clip(entries, min=-reach, max=reach).astype(kind)


def setup_inputs(seed: int = 0) -> dict:
    seeds = jax.random.split(jax.random.key(seed), 7)
    return {
        "samples": draw_samples(jax.random.fold_in(seeds[6], 71), 0),
        "loadings": draw_loadings(jax.random.fold_in(seeds[6], 71), 0),
        "omega_tiles": gaussian(seeds[2], (TILES, BS, BS), 0.03, 0.18, ((0, 256),), jnp.float32),
        "omega_diagonal": jnp.clip(jnp.exp(math.log(2.0) - 1.3862944 * jax.random.uniform(seeds[3], (P_SIZE,), jnp.float32) ** block_levels(seeds[3], (P_SIZE,), ((0, 32),), -0.2, 0.2)), 0.5, 2.0),
        "tile_rows": draw_tile_rows(jax.random.fold_in(seeds[6], 71), 0),
        "tile_cols": draw_tile_cols(jax.random.fold_in(seeds[6], 71), 0),
    }


step_size = 0.5
penalty = 0.02


def reference(samples, loadings, omega_tiles, omega_diagonal, tile_rows, tile_cols):
    highest = lax.Precision.HIGHEST
    factor_load = loadings.astype(jnp.float32)
    scores = jnp.dot(samples, factor_load.T, precision=highest, preferred_element_type=jnp.float32)
    residual = samples - jnp.dot(scores, factor_load, precision=highest, preferred_element_type=jnp.float32)
    diagonal_mask = jnp.eye(BS, dtype=bool)

    def apply_tile(running, tile_entry):
        tile_block, row_block, col_block = tile_entry
        keep_mask = jnp.where((row_block == col_block) & diagonal_mask, 0.0, 1.0)
        source = lax.dynamic_slice_in_dim(residual, (col_block * BS).astype(jnp.int32), BS, 1)
        product = jnp.dot(source, (tile_block * keep_mask).T, precision=highest, preferred_element_type=jnp.float32)
        row_start = (row_block * BS).astype(jnp.int32)
        current = lax.dynamic_slice_in_dim(running, row_start, BS, 1)
        return lax.dynamic_update_slice_in_dim(running, current + product, row_start, 1), None

    applied, _ = lax.scan(apply_tile, residual * omega_diagonal, (omega_tiles, tile_rows, tile_cols))

    def tile_step(tile_entry):
        tile_block, row_block, col_block = tile_entry
        keep_mask = jnp.where((row_block == col_block) & diagonal_mask, 0.0, 1.0)
        row_start = (row_block * BS).astype(jnp.int32)
        col_start = (col_block * BS).astype(jnp.int32)
        rows_applied = lax.dynamic_slice_in_dim(applied, row_start, BS, 1)
        rows_resid = lax.dynamic_slice_in_dim(residual, row_start, BS, 1)
        cols_applied = lax.dynamic_slice_in_dim(applied, col_start, BS, 1)
        cols_resid = lax.dynamic_slice_in_dim(residual, col_start, BS, 1)
        first_term = jnp.dot(rows_applied.T, cols_resid, precision=highest, preferred_element_type=jnp.float32)
        second = jnp.dot(rows_resid.T, cols_applied, precision=highest, preferred_element_type=jnp.float32)
        gradient = 0.5 * (first_term + second) / NS
        stepped = (tile_block - step_size * gradient) * keep_mask
        return jnp.sign(stepped) * jnp.maximum(jnp.abs(stepped) - step_size * penalty, 0.0)

    new_tiles = lax.map(tile_step, (omega_tiles, tile_rows, tile_cols))
    diag_stat = jnp.sum(applied * residual, axis=0) / NS
    new_diagonal = omega_diagonal - step_size * (diag_stat - 1.0 / omega_diagonal)
    return new_tiles, new_diagonal
```

```python
import functools
import jax
import jax.numpy as jnp
from jax import lax
from jax.experimental import pallas as pl
from jax.experimental.pallas import tpu as pltpu
from jax.sharding import PartitionSpec as P

step_size = 0.5
penalty = 0.02
MESH = pl.DeviceIdType.MESH
CAP = 3
Y = 4
Z = 8
C = 8
BLK = 8
TD = 5
NC = 2
SC = 8
BS = 512
PLANE = Z * BLK
SLOTS = Z * CAP

PICK = 0
FWD = PICK + (Y - 1) * SLOTS
ORDER = FWD + C * TD
SAME = ORDER + C * TD
LAST = SAME + C * TD
HAS = LAST + BLK
DIAG = HAS + BLK
META = DIAG + TD


def split2(x):
    hi = x.astype(jnp.bfloat16)
    return hi, (x - hi.astype(jnp.float32)).astype(jnp.bfloat16)


def split3(x):
    hi, rest = x.astype(jnp.bfloat16), None
    rest = x - hi.astype(jnp.float32)
    mid, low = split2(rest)
    return jnp.concatenate([hi, mid, low], axis=0)


def dot(a, b, dims):
    return lax.dot_general(a, b, (dims, ((), ())), preferred_element_type=jnp.float32)


def wait_all(ref, sem):
    pltpu.make_async_copy(ref, ref, sem).wait()


def route_kernel(
    meta,
    samples,
    loadings,
    diag,
    tiles,
    routed_out,
    group_out,
    diag_out,
    part,
    score_z,
    score_y,
    stage,
    seg,
    tile_f32,
    tile_hi,
    tile_lo,
    group,
    *rest,
):
    n = 2 * NC
    pair = lambda flat: (flat[:NC], flat[NC:])
    field, ysend, fsend, frecv = (pair(rest[i * n : (i + 1) * n]) for i in range(4))
    rest = rest[4 * n :]
    psend, precv = rest[:NC], rest[NC : 2 * NC]
    (
        exch_s,
        exch_r,
        ring_s,
        ring_r,
        y_s,
        y_r,
        f_s,
        f_r,
        p_s,
        p_r,
        g_s,
        g_r,
        local,
    ) = rest[2 * NC :]

    row = lax.axis_index("rows")
    me = lax.axis_index("cols")
    y, z = row // Z, row % Z
    at_z = lambda d: {"rows": y * Z + (z + d + Z) % Z}
    at_y = lambda d: {"rows": ((y + d) % Y) * Z + z}
    at_c = lambda d: {"cols": (me + d + C) % C}

    def remote(src, dst, send, recv, where):
        return pltpu.make_async_remote_copy(
            src_ref=src,
            dst_ref=dst,
            send_sem=send,
            recv_sem=recv,
            device_id=where,
            device_id_type=MESH,
        )

    def each(low, high, body):
        lax.fori_loop(low, high, lambda i, _: (body(i), None)[1], None)

    barrier = pltpu.get_barrier_semaphore()

    def greet(where, count):
        each(
            1,
            count,
            lambda d: pl.semaphore_signal(
                barrier, inc=1, device_id=where(d), device_id_type=MESH
            ),
        )

    greet(at_z, Z)
    greet(at_y, Y)
    greet(at_c, C)
    tile_copy = pltpu.make_async_copy(tiles, tile_f32, local.at[0])
    tile_copy.start()

    def score_step(b, total):
        cols = pl.ds(pl.multiple_of(b * BS, BS), BS)
        return total + dot(split3(samples[:, cols]), loadings[:, cols], ((1,), (1,)))

    ns = NC * SC
    total = lax.fori_loop(0, BLK, score_step, jnp.zeros((3 * ns, loadings.shape[0]), jnp.float32))
    part[0] = total[:ns] + total[ns : 2 * ns] + total[2 * ns :]
    pl.semaphore_wait(barrier, Z + Y + C - 3)

    each(
        1,
        Z,
        lambda d: remote(part.at[0], score_z.at[d], exch_s.at[0], exch_r.at[0], at_z(d)).start(),
    )
    wait_all(score_z.at[pl.ds(1, Z - 1)], exch_r.at[0])
    total = part[0]
    for d in range(1, Z):
        total = total + score_z[d]
    part[1] = total
    each(
        1,
        Y,
        lambda d: remote(part.at[1], score_y.at[d], exch_s.at[1], exch_r.at[1], at_y(d)).start(),
    )
    wait_all(score_y.at[pl.ds(1, Y - 1)], exch_r.at[1])
    for d in range(1, Y):
        total = total + score_y[d]
    scores = split3(total)

    def residual_step(b):
        cols = pl.ds(pl.multiple_of(b * BS, BS), BS)
        terms = dot(scores, loadings[:, cols], ((1,), (0,)))
        value = samples[:, cols] - (terms[:ns] + terms[ns : 2 * ns] + terms[2 * ns :])
        for h in range(NC):
            field[0][h][z * BLK + b] = value[h * SC : (h + 1) * SC]
            group[0, h, 0, b] = value[h * SC : (h + 1) * SC]

    each(0, BLK, residual_step)

    def hop(p, h, k, right):
        slice_of = ((z - k + 1 + Z) if right else (z + k - 1)) % Z
        ref = field[p][h]
        last = isinstance(k, int) and k == Z // 2
        low = slice_of * BLK + (0 if right or not last else BLK // 2)
        where = pl.ds(low, BLK // 2 if last else BLK)
        way = 0 if right else 1
        return remote(
            ref.at[where],
            ref.at[where],
            ring_s.at[p, h, way],
            ring_r.at[p, h, way, k],
            at_z(1 if right else -1),
        )

    def arrived(p, h, k, right):
        slice_of = ((z - k + Z) if right else (z + k)) % Z
        last = isinstance(k, int) and k == Z // 2
        low = slice_of * BLK + (0 if right or not last else BLK // 2)
        ref = field[p][h].at[pl.ds(low, BLK // 2 if last else BLK)]
        wait_all(ref, ring_r.at[p, h, 0 if right else 1, k])

    def send_picks(p, h, zs):
        ref = field[p][h]
        stage[...] = ref[pl.ds(zs * BLK, BLK)]

        def to_plane(i):
            base = i * SLOTS + zs * CAP
            for j in range(CAP):
                ysend[p][h][base + j] = stage[meta[PICK + base + j]]
            remote(
                ysend[p][h].at[pl.ds(base, CAP)],
                ref.at[pl.ds(PLANE + base, CAP)],
                y_s.at[p, h, i],
                y_r.at[p, h, i],
                at_y(i + 1),
            ).start()

        each(0, Y - 1, to_plane)

    def route(p, h, first=None, middle=None):
        hop(p, h, 1, True).start()
        hop(p, h, 1, False).start()
        send_picks(p, h, z)
        if first:
            first()

        def step(k):
            arrived(p, h, k, True)
            hop(p, h, k + 1, True).start()
            arrived(p, h, k, False)
            hop(p, h, k + 1, False).start()
            send_picks(p, h, (z - k + Z) % Z)
            send_picks(p, h, (z + k) % Z)

        each(1, Z // 2 - 1, step)
        step(Z // 2 - 1)
        if middle:
            middle()
        arrived(p, h, Z // 2, True)
        arrived(p, h, Z // 2, False)
        send_picks(p, h, (z + Z // 2) % Z)
        for i in range(Y - 1):
            wait_all(field[p][h].at[pl.ds(PLANE + i * SLOTS, SLOTS)], y_r.at[p, h, i])

    def forward(p, h):
        def one(d):
            dest = (me + d) % C
            for t in range(TD):
                fsend[p][h][d, t] = field[p][h][meta[FWD + dest * TD + t]]
            remote(
                fsend[p][h].at[d],
                frecv[p][h].at[d],
                f_s.at[p, h],
                f_r.at[p, h],
                at_c(d),
            ).start()

        each(1, C, one)
        for t in range(TD):
            frecv[p][h][0, t] = field[p][h][meta[FWD + me * TD + t]]

    def forwarded(p, h):
        wait_all(frecv[p][h].at[pl.ds(1, C - 1)], f_r.at[p, h])

    def gather_start(p, h):
        each(
            1,
            C,
            lambda d: remote(
                group.at[p, h, 0], group.at[p, h, d], g_s.at[p, h], g_r.at[p, h], at_c(d)
            ).start(),
        )

    def split_tiles():
        tile_copy.wait()
        rows = lax.broadcasted_iota(jnp.int32, (BS // 4, BS), 0)
        cols = lax.broadcasted_iota(jnp.int32, (BS // 4, BS), 1)

        def one(i):
            t, q = i // 4, i % 4
            at = pl.ds(pl.multiple_of(q * (BS // 4), BS // 4), BS // 4)
            flag = jnp.full((BS // 4, BS), meta[DIAG + t], jnp.int32)
            drop = (rows + q * (BS // 4) == cols) & (flag != 0)
            hi, lo = split2(jnp.where(drop, 0.0, tile_f32[t, at]))
            tile_hi[t, at] = hi
            tile_lo[t, at] = lo

        each(0, TD * 4, one)

    def products(h):
        forwarded(0, h)

        def one(t):
            hi, lo = split2(frecv[0][h][:, t].reshape(C * SC, BS))
            both = dot(jnp.concatenate([hi, lo], axis=0), tile_hi[t], ((1,), (1,)))
            value = both[: C * SC] + both[C * SC :] + dot(hi, tile_lo[t], ((1,), (1,)))
            value = value.reshape(C, SC, BS)
            for d in range(C):
                psend[h][d * TD + t] = value[d]

        each(0, TD, one)
        each(
            1,
            C,
            lambda d: remote(
                psend[h].at[pl.ds(d * TD, TD)],
                precv[h].at[pl.ds(d * TD, TD)],
                p_s.at[h],
                p_r.at[h],
                at_c(-d),
            ).start(),
        )
        for t in range(TD):
            precv[h][t] = psend[h][t]

    def apply_rows(h):
        wait_all(precv[h].at[pl.ds(TD, (C - 1) * TD)], p_r.at[h])

        def one(k, running):
            same = jnp.full((SC, BS), meta[SAME + k], jnp.int32) != 0
            running = jnp.where(same, running, 0.0) + precv[h][meta[ORDER + k]]
            seg[k] = running
            return running

        lax.fori_loop(0, C * TD, one, jnp.zeros((SC, BS), jnp.float32))

        def block(b):
            has = jnp.full((SC, BS), meta[HAS + b], jnp.int32) != 0
            value = jnp.where(has, seg[meta[LAST + b]], 0.0)
            value = value + diag[pl.ds(b, 1)] * group[0, h, 0, b]
            field[1][h][z * BLK + b] = value
            group[1, h, 0, b] = value

        each(0, BLK, block)

    def start_gathers():
        for h in range(NC):
            gather_start(0, h)

    route(0, 0, first=start_gathers, middle=split_tiles)
    forward(0, 0)
    route(0, 1, middle=lambda: products(0))
    forward(0, 1)
    apply_rows(0)
    route(1, 0, first=lambda: gather_start(1, 0), middle=lambda: products(1))
    forward(1, 0)
    apply_rows(1)
    route(1, 1, first=lambda: gather_start(1, 1))
    forward(1, 1)

    def out_copy(src, dst):
        copy = pltpu.make_async_copy(src, dst, local.at[1])
        copy.start()

    for p in range(2):
        for h in range(NC):
            wait_all(group.at[p, h, pl.ds(1, C - 1)], g_r.at[p, h])
    out_copy(group, group_out)

    def diag_step(b):
        total = jnp.zeros((SC, BS), jnp.float32)
        for h in range(NC):
            for d in range(C):
                total = total + group[0, h, d, b] * group[1, h, d, b]
        stat = jnp.sum(total, axis=0, keepdims=True) / (NC * C * SC)
        old = diag[pl.ds(b, 1)]
        diag_out[pl.ds(b, 1)] = old - step_size * (stat - 1.0 / old)

    each(0, BLK, diag_step)
    for p in range(2):
        for h in range(NC):
            if p == 1:
                forwarded(p, h)
            copy = pltpu.make_async_copy(frecv[p][h], routed_out.at[p, h], local.at[2 + p * NC + h])
            copy.start()

    wait_all(score_z.at[pl.ds(1, Z - 1)], exch_s.at[0])
    wait_all(score_y.at[pl.ds(1, Y - 1)], exch_s.at[1])
    sent = Z // 2 * BLK - BLK // 2
    for p in range(2):
        for h in range(NC):
            for way in range(2):
                wait_all(field[p][h].at[pl.ds(0, sent)], ring_s.at[p, h, way])
            for i in range(Y - 1):
                wait_all(ysend[p][h].at[pl.ds(i * SLOTS, SLOTS)], y_s.at[p, h, i])
            wait_all(fsend[p][h].at[pl.ds(1, C - 1)], f_s.at[p, h])
            wait_all(group.at[p, h, pl.ds(1, C - 1)], g_s.at[p, h])
    for h in range(NC):
        wait_all(psend[h].at[pl.ds(TD, (C - 1) * TD)], p_s.at[h])
    pltpu.make_async_copy(group, group_out, local.at[1]).wait()
    for p in range(2):
        for h in range(NC):
            pltpu.make_async_copy(
                frecv[p][h], routed_out.at[p, h], local.at[2 + p * NC + h]
            ).wait()


def step_kernel(info, routed, rows, tile, out):
    t = pl.program_id(0)
    samples = NC * C * SC
    flat = lambda ref, p: ref[p].reshape(samples, BS)
    left = jnp.concatenate([flat(rows, 1), flat(rows, 0)], axis=0)
    right = jnp.concatenate([flat(routed, 0), flat(routed, 1)], axis=0)
    left_hi, left_lo = split2(left)
    right_hi, right_lo = split2(right)
    dims = ((0,), (0,))
    total = dot(left_hi, right_hi, dims) + dot(left_hi, right_lo, dims) + dot(left_lo, right_hi, dims)
    stepped = tile[0] - (step_size * 0.5 / samples) * total
    i = lax.broadcasted_iota(jnp.int32, (BS, BS), 0)
    j = lax.broadcasted_iota(jnp.int32, (BS, BS), 1)
    flag = jnp.full((BS, BS), info[TD + t], jnp.int32)
    stepped = jnp.where((i == j) & (flag != 0), 0.0, stepped)
    limit = step_size * penalty
    out[0] = stepped - jnp.clip(stepped, -limit, limit)


def index_table(tile_rows, tile_cols, row, me):
    y, z = row // Z, row % Z
    groups = Y * Z
    tiles = C * TD
    wanted = ((y + jnp.arange(Y)) % Y) * Z + z
    take = wanted[:, None, None] == jnp.arange(groups)[None, :, None]
    cols = jnp.sum(jnp.where(take, tile_cols.reshape(1, groups, tiles), 0), axis=1)
    rows = jnp.sum(jnp.where(take[0], tile_rows.reshape(groups, tiles), 0), axis=0)
    source, local = cols // BLK, cols % BLK
    place = jnp.arange(tiles)
    rank = jnp.sum(
        (source[:, :, None] == source[:, None, :]) & (place[None, :] < place[:, None])[None],
        axis=2,
        dtype=jnp.int32,
    )
    slot = jnp.arange(SLOTS)
    chosen = (source[1:, None, :] == y * Z + slot[None, :, None] // CAP) & (
        rank[1:, None, :] == slot[None, :, None] % CAP
    )
    pick = jnp.sum(jnp.where(chosen, local[1:, None, :], 0), axis=2).reshape(-1)
    plane, depth = source[0] // Z, source[0] % Z
    away = (y - plane + Y) % Y
    fwd = jnp.where(
        away == 0,
        depth * BLK + local[0],
        PLANE + (away - 1) * SLOTS + depth * CAP + rank[0],
    )
    local_rows = rows - row * BLK
    before = (local_rows[None, :] < local_rows[:, None]) | (
        (local_rows[None, :] == local_rows[:, None]) & (place[None, :] < place[:, None])
    )
    position = jnp.sum(before, axis=1, dtype=jnp.int32)
    at = position[None, :] == place[:, None]
    lands = ((place // TD - me + C) % C) * TD + place % TD
    order = jnp.sum(jnp.where(at, lands[None, :], 0), axis=1)
    first = jnp.sum(local_rows[None, :] < local_rows[:, None], axis=1, dtype=jnp.int32)
    same = jnp.sum(jnp.where(at, (position > first)[None, :].astype(jnp.int32), 0), axis=1)
    blocks = jnp.arange(BLK)
    upto = jnp.sum(local_rows[None, :] <= blocks[:, None], axis=1, dtype=jnp.int32)
    count = jnp.sum(local_rows[None, :] == blocks[:, None], axis=1, dtype=jnp.int32)
    mine = (me * TD + jnp.arange(TD))[:, None] == place[None, :]
    my_rows = jnp.sum(jnp.where(mine, local_rows[None, :], 0), axis=1)
    on_diag = jnp.sum(jnp.where(mine, (rows == cols[0])[None, :].astype(jnp.int32), 0), axis=1)
    table = jnp.concatenate(
        [pick, fwd, order, same, jnp.maximum(upto - 1, 0), (count > 0).astype(jnp.int32), on_diag]
    )
    return table.astype(jnp.int32), jnp.concatenate([my_rows, on_diag]).astype(jnp.int32)


def per_device(samples, loadings, omega_tiles, omega_diagonal, tile_rows, tile_cols):
    row = lax.axis_index("rows")
    me = lax.axis_index("cols")
    factors = loadings.shape[0]
    ns = NC * SC
    table, info = index_table(tile_rows, tile_cols, row, me)
    f32 = jnp.float32
    vmem = lambda *shape: pltpu.VMEM(shape, f32)
    dma = lambda *shape: pltpu.SemaphoreType.DMA(shape)
    in_vmem = pl.BlockSpec(memory_space=pltpu.VMEM)
    anywhere = pl.BlockSpec(memory_space=pl.ANY)
    n = 2 * NC
    routed, group, new_diagonal = pl.pallas_call(
        route_kernel,
        out_shape=(
            jax.ShapeDtypeStruct((2, NC, C, TD, SC, BS), f32),
            jax.ShapeDtypeStruct((2, NC, C, BLK, SC, BS), f32),
            jax.ShapeDtypeStruct((BLK, BS), f32),
        ),
        in_specs=[
            pl.BlockSpec(memory_space=pltpu.SMEM),
            in_vmem,
            in_vmem,
            in_vmem,
            anywhere,
        ],
        out_specs=(anywhere, anywhere, in_vmem),
        scratch_shapes=[
            vmem(2, ns, factors),
            vmem(Z, ns, factors),
            vmem(Y, ns, factors),
            vmem(BLK, SC, BS),
            vmem(C * TD, SC, BS),
            vmem(TD, BS, BS),
            pltpu.VMEM((TD, BS, BS), jnp.bfloat16),
            pltpu.VMEM((TD, BS, BS), jnp.bfloat16),
            vmem(2, NC, C, BLK, SC, BS),
        ]
        + [vmem(PLANE + (Y - 1) * SLOTS, SC, BS)] * n
        + [vmem((Y - 1) * SLOTS, SC, BS)] * n
        + [vmem(C, TD, SC, BS)] * n
        + [vmem(C, TD, SC, BS)] * n
        + [vmem(C * TD, SC, BS)] * NC
        + [vmem(C * TD, SC, BS)] * NC
        + [
            dma(2),
            dma(2),
            dma(2, NC, 2),
            dma(2, NC, 2, Z // 2 + 1),
            dma(2, NC, Y - 1),
            dma(2, NC, Y - 1),
            dma(2, NC),
            dma(2, NC),
            dma(NC),
            dma(NC),
            dma(2, NC),
            dma(2, NC),
            dma(2 + n),
        ],
        compiler_params=pltpu.CompilerParams(
            collective_id=0, has_side_effects=True, vmem_limit_bytes=56 * 1024 * 1024
        ),
        name="route",
    )(table, samples, loadings, omega_diagonal.reshape(BLK, BS), omega_tiles)

    new_tiles = pl.pallas_call(
        step_kernel,
        out_shape=jax.ShapeDtypeStruct(omega_tiles.shape, f32),
        grid_spec=pltpu.PrefetchScalarGridSpec(
            num_scalar_prefetch=1,
            grid=(TD,),
            in_specs=[
                pl.BlockSpec((2, NC, C, None, SC, BS), lambda t, info: (0, 0, 0, t, 0, 0)),
                pl.BlockSpec((2, NC, C, None, SC, BS), lambda t, info: (0, 0, 0, info[t], 0, 0)),
                pl.BlockSpec((1, BS, BS), lambda t, info: (t, 0, 0)),
            ],
            out_specs=pl.BlockSpec((1, BS, BS), lambda t, info: (t, 0, 0)),
        ),
        compiler_params=pltpu.CompilerParams(vmem_limit_bytes=32 * 1024 * 1024),
        name="step",
    )(info, routed, group, omega_tiles)
    return new_tiles, new_diagonal.reshape(-1)


def solution(mesh):
    placed = (
        P("cols", "rows"),
        P(None, "rows"),
        P(("rows", "cols"), None, None),
        P("rows"),
        P(),
        P(),
    )
    return jax.shard_map(
        per_device,
        mesh=mesh,
        in_specs=placed,
        out_specs=(P(("rows", "cols"), None, None), P("rows")),
        check_vma=False,
    )
```

```python
import functools
import jax
import jax.numpy as jnp
from jax import lax
from jax.experimental import pallas as pl
from jax.experimental.pallas import tpu as pltpu
from jax.sharding import PartitionSpec as P

step_size = 0.5
penalty = 0.02
MESH = pl.DeviceIdType.MESH
CAP = 3
Y = 4
Z = 8
C = 8
BLK = 8
TD = 5
NC = 2
SC = 8
BS = 512
PLANE = Z * BLK
SLOTS = Z * CAP

PICK = 0
FWD = PICK + (Y - 1) * SLOTS
ORDER = FWD + C * TD
SAME = ORDER + C * TD
LAST = SAME + C * TD
HAS = LAST + BLK
DIAG = HAS + BLK
META = DIAG + TD


def split2(x):
    hi = x.astype(jnp.bfloat16)
    return hi, (x - hi.astype(jnp.float32)).astype(jnp.bfloat16)


def split3(x):
    hi, rest = x.astype(jnp.bfloat16), None
    rest = x - hi.astype(jnp.float32)
    mid, low = split2(rest)
    return jnp.concatenate([hi, mid, low], axis=0)


def dot(a, b, dims):
    return lax.dot_general(a, b, (dims, ((), ())), preferred_element_type=jnp.float32)


def wait_all(ref, sem):
    pltpu.make_async_copy(ref, ref, sem).wait()


def route_kernel(
    meta,
    samples,
    loadings,
    diag,
    tiles,
    routed_out,
    group_out,
    diag_out,
    part,
    score_z,
    score_y,
    score_c,
    window,
    stage,
    seg,
    tile_f32,
    tile_hi,
    tile_lo,
    group,
    *rest,
):
    n = 2 * NC
    pair = lambda flat: (flat[:NC], flat[NC:])
    field, ysend, fsend, frecv = (pair(rest[i * n : (i + 1) * n]) for i in range(4))
    rest = rest[4 * n :]
    psend, precv = rest[:NC], rest[NC : 2 * NC]
    (
        exch_s,
        exch_r,
        ring_s,
        ring_r,
        y_s,
        y_r,
        f_s,
        f_r,
        p_s,
        p_r,
        g_s,
        g_r,
        h_s,
        h_r,
        w_s,
        w_r,
        v_s,
        v_r,
        local,
    ) = rest[2 * NC :]

    row = lax.axis_index("rows")
    me = lax.axis_index("cols")
    y, z = row // Z, row % Z
    at_z = lambda d: {"rows": y * Z + (z + d + Z) % Z}
    at_y = lambda d: {"rows": ((y + d) % Y) * Z + z}
    at_c = lambda d: {"cols": (me + d + C) % C}
    side = 1 - 2 * (me % 2)
    other = at_c(side)

    def remote(src, dst, send, recv, where):
        return pltpu.make_async_remote_copy(
            src_ref=src,
            dst_ref=dst,
            send_sem=send,
            recv_sem=recv,
            device_id=where,
            device_id_type=MESH,
        )

    def each(low, high, body):
        lax.fori_loop(low, high, lambda i, _: (body(i), None)[1], None)

    barrier = pltpu.get_barrier_semaphore()

    def greet(where, count):
        each(
            1,
            count,
            lambda d: pl.semaphore_signal(
                barrier, inc=1, device_id=where(d), device_id_type=MESH
            ),
        )

    greet(at_z, Z)
    greet(at_y, Y)
    greet(at_c, C)
    tile_copy = pltpu.make_async_copy(tiles, tile_f32, local.at[0])
    tile_copy.start()

    def split_tiles(low, high):
        rows = lax.broadcasted_iota(jnp.int32, (BS // 4, BS), 0)
        cols = lax.broadcasted_iota(jnp.int32, (BS // 4, BS), 1)

        def one(i):
            t, q = i // 4, i % 4
            at = pl.ds(pl.multiple_of(q * (BS // 4), BS // 4), BS // 4)
            flag = jnp.full((BS // 4, BS), meta[DIAG + t], jnp.int32)
            drop = (rows + q * (BS // 4) == cols) & (flag != 0)
            hi, lo = split2(jnp.where(drop, 0.0, tile_f32[t, at]))
            tile_hi[t, at] = hi
            tile_lo[t, at] = lo

        each(low, high, one)

    def score_step(b, total):
        cols = pl.ds(pl.multiple_of(b * BS, BS), BS)
        return total + dot(split3(samples[:, cols]), loadings[:, cols], ((1,), (1,)))

    ns = NC * SC
    total = lax.fori_loop(0, BLK, score_step, jnp.zeros((3 * ns, loadings.shape[0]), jnp.float32))
    part[0] = total[:ns] + total[ns : 2 * ns] + total[2 * ns :]
    pl.semaphore_wait(barrier, Z + Y + C - 3)

    def gather_start(src, place, far_s, far_r, near_s, near_r):
        each(
            1,
            C // 2,
            lambda q: remote(src, place(2 * q), far_s.at[q], far_r.at[q], at_c(2 * q)).start(),
        )
        remote(src, place((side + C) % C), near_s.at[0], near_r.at[0], other).start()

    def gather_pass(place, far_r, near_s, near_r):
        def one(q):
            wait_all(place(2 * q), far_r.at[q])
            remote(
                place(2 * q), place((side + 2 * q + C) % C), near_s.at[q], near_r.at[q], other
            ).start()

        each(1, C // 2, one)

    def gathered(place, near_r):
        each(0, C // 2, lambda q: wait_all(place((2 * q - side + C) % C), near_r.at[q]))

    def gather_sent(place, far_s, near_s):
        each(1, C // 2, lambda q: wait_all(place(2 * q), far_s.at[q]))
        each(0, C // 2, lambda q: wait_all(place(2 * q), near_s.at[q]))

    window_at = lambda d: window.at[d]

    each(
        1,
        Z,
        lambda d: remote(part.at[0], score_z.at[d], exch_s.at[0], exch_r.at[0], at_z(d)).start(),
    )
    gather_start(samples, window_at, w_s, w_r, v_s, v_r)
    tile_copy.wait()
    split_tiles(0, 12)
    wait_all(score_z.at[pl.ds(1, Z - 1)], exch_r.at[0])
    total = part[0]
    for d in range(1, Z):
        total = total + score_z[d]
    part[1] = total
    each(
        1,
        Y,
        lambda d: remote(part.at[1], score_y.at[d], exch_s.at[1], exch_r.at[1], at_y(d)).start(),
    )
    split_tiles(12, TD * 4)
    wait_all(score_y.at[pl.ds(1, Y - 1)], exch_r.at[1])
    for d in range(1, Y):
        total = total + score_y[d]
    scores = split3(total)
    part[2] = total

    def residual_step(b):
        cols = pl.ds(pl.multiple_of(b * BS, BS), BS)
        terms = dot(scores, loadings[:, cols], ((1,), (0,)))
        value = samples[:, cols] - (terms[:ns] + terms[ns : 2 * ns] + terms[2 * ns :])
        for h in range(NC):
            field[0][h][z * BLK + b] = value[h * SC : (h + 1) * SC]
            group[0, h, 0, b] = value[h * SC : (h + 1) * SC]

    each(0, BLK, residual_step)

    def group_residual():
        gathered(window_at, v_r)
        wait_all(score_c.at[pl.ds(1, C - 1)], exch_r.at[2])
        far = (C - 1) * ns
        terms3 = split3(score_c[1:].reshape(far, loadings.shape[0]))

        def one(b):
            cols = pl.ds(pl.multiple_of(b * BS, BS), BS)
            terms = dot(terms3, loadings[:, cols], ((1,), (0,)))
            terms = terms[:far] + terms[far : 2 * far] + terms[2 * far :]
            value = window[pl.ds(1, C - 1), :, cols] - terms.reshape(C - 1, ns, BS)
            for h in range(NC):
                group[0, h, pl.ds(1, C - 1), b] = value[:, h * SC : (h + 1) * SC]

        each(0, BLK, one)

    def hop(p, h, k, right):
        slice_of = ((z - k + 1 + Z) if right else (z + k - 1)) % Z
        ref = field[p][h]
        last = isinstance(k, int) and k == Z // 2
        low = slice_of * BLK + (0 if right or not last else BLK // 2)
        where = pl.ds(low, BLK // 2 if last else BLK)
        way = 0 if right else 1
        return remote(
            ref.at[where],
            ref.at[where],
            ring_s.at[p, h, way],
            ring_r.at[p, h, way, k],
            at_z(1 if right else -1),
        )

    def arrived(p, h, k, right):
        slice_of = ((z - k + Z) if right else (z + k)) % Z
        last = isinstance(k, int) and k == Z // 2
        low = slice_of * BLK + (0 if right or not last else BLK // 2)
        ref = field[p][h].at[pl.ds(low, BLK // 2 if last else BLK)]
        wait_all(ref, ring_r.at[p, h, 0 if right else 1, k])

    def send_picks(p, h, zs):
        ref = field[p][h]
        stage[...] = ref[pl.ds(zs * BLK, BLK)]

        def to_plane(i):
            base = i * SLOTS + zs * CAP
            for j in range(CAP):
                ysend[p][h][base + j] = stage[meta[PICK + base + j]]
            remote(
                ysend[p][h].at[pl.ds(base, CAP)],
                ref.at[pl.ds(PLANE + base, CAP)],
                y_s.at[p, h, i],
                y_r.at[p, h, i],
                at_y(i + 1),
            ).start()

        each(0, Y - 1, to_plane)

    def ring_start(p, h):
        hop(p, h, 1, True).start()
        hop(p, h, 1, False).start()

    def ring_step(p, h, k):
        arrived(p, h, k, True)
        hop(p, h, k + 1, True).start()
        arrived(p, h, k, False)
        hop(p, h, k + 1, False).start()

    def ring_end(p, h):
        arrived(p, h, Z // 2, True)
        arrived(p, h, Z // 2, False)

    def picks_at(p, h, k):
        send_picks(p, h, (z - k + Z) % Z)
        send_picks(p, h, (z + k) % Z)

    def routed(p, h):
        for i in range(Y - 1):
            wait_all(field[p][h].at[pl.ds(PLANE + i * SLOTS, SLOTS)], y_r.at[p, h, i])

    def forward(p, h):
        def one(d):
            dest = (me + d) % C
            for t in range(TD):
                fsend[p][h][d, t] = field[p][h][meta[FWD + dest * TD + t]]
            remote(
                fsend[p][h].at[d],
                frecv[p][h].at[d],
                f_s.at[p, h],
                f_r.at[p, h],
                at_c(d),
            ).start()

        each(1, C, one)
        for t in range(TD):
            frecv[p][h][0, t] = field[p][h][meta[FWD + me * TD + t]]

    def forwarded(p, h):
        wait_all(frecv[p][h].at[pl.ds(1, C - 1)], f_r.at[p, h])

    def products(h):
        forwarded(0, h)

        def one(t):
            hi, lo = split2(frecv[0][h][:, t].reshape(C * SC, BS))
            both = dot(jnp.concatenate([hi, lo], axis=0), tile_hi[t], ((1,), (1,)))
            value = both[: C * SC] + both[C * SC :] + dot(hi, tile_lo[t], ((1,), (1,)))
            value = value.reshape(C, SC, BS)
            precv[h][t] = value[0]
            for d in range(1, C):
                psend[h][d * TD + t] = value[d]
            each(
                1,
                C,
                lambda d: remote(
                    psend[h].at[d * TD + t],
                    precv[h].at[d * TD + t],
                    p_s.at[h],
                    p_r.at[h],
                    at_c(-d),
                ).start(),
            )

        each(0, TD, one)

    def apply_rows(h):
        wait_all(precv[h].at[pl.ds(TD, (C - 1) * TD)], p_r.at[h])

        def one(k, running):
            same = jnp.full((SC, BS), meta[SAME + k], jnp.int32) != 0
            running = jnp.where(same, running, 0.0) + precv[h][meta[ORDER + k]]
            seg[k] = running
            return running

        lax.fori_loop(0, C * TD, one, jnp.zeros((SC, BS), jnp.float32))

        def block(b):
            has = jnp.full((SC, BS), meta[HAS + b], jnp.int32) != 0
            value = jnp.where(has, seg[meta[LAST + b]], 0.0)
            value = value + diag[pl.ds(b, 1)] * group[0, h, 0, b]
            field[1][h][z * BLK + b] = value
            group[1, h, 0, b] = value

        each(0, BLK, block)

    group_at = lambda h: lambda d: group.at[1, h, d]

    def rows_start(h):
        gather_start(group.at[1, h, 0], group_at(h), g_s.at[h], g_r.at[h], h_s.at[h], h_r.at[h])

    def rows_pass(h):
        gather_pass(group_at(h), g_r.at[h], h_s.at[h], h_r.at[h])

    ring_start(0, 0)
    send_picks(0, 0, z)
    ring_start(0, 1)
    send_picks(0, 1, z)
    each(
        1,
        C,
        lambda d: remote(part.at[2], score_c.at[d], exch_s.at[2], exch_r.at[2], at_c(d)).start(),
    )

    def both(k):
        ring_step(0, 0, k)
        picks_at(0, 0, k)
        ring_step(0, 1, k)

    each(1, Z // 2 - 1, both)
    both(Z // 2 - 1)
    gather_pass(window_at, w_r, v_s, v_r)
    ring_end(0, 0)
    send_picks(0, 0, (z + Z // 2) % Z)
    each(1, Z // 2, lambda k: picks_at(0, 1, k))
    ring_end(0, 1)
    send_picks(0, 1, (z + Z // 2) % Z)
    group_residual()
    routed(0, 0)
    forward(0, 0)
    products(0)
    routed(0, 1)
    forward(0, 1)

    apply_rows(0)
    ring_start(1, 0)
    send_picks(1, 0, z)
    rows_start(0)
    ring_step(1, 0, 1)
    picks_at(1, 0, 1)
    ring_step(1, 0, 2)
    picks_at(1, 0, 2)
    products(1)
    ring_step(1, 0, 3)
    picks_at(1, 0, 3)
    ring_end(1, 0)
    send_picks(1, 0, (z + Z // 2) % Z)
    rows_pass(0)
    apply_rows(1)
    ring_start(1, 1)
    send_picks(1, 1, z)
    rows_start(1)
    ring_step(1, 1, 1)
    picks_at(1, 1, 1)
    ring_step(1, 1, 2)
    picks_at(1, 1, 2)
    routed(1, 0)
    forward(1, 0)
    ring_step(1, 1, 3)
    picks_at(1, 1, 3)
    ring_end(1, 1)
    send_picks(1, 1, (z + Z // 2) % Z)
    rows_pass(1)
    for h in range(NC):
        gathered(group_at(h), h_r.at[h])
    routed(1, 1)
    forward(1, 1)

    def out_copy(src, dst):
        copy = pltpu.make_async_copy(src, dst, local.at[1])
        copy.start()

    out_copy(group, group_out)

    def diag_step(b):
        total = jnp.zeros((SC, BS), jnp.float32)
        for h in range(NC):
            for d in range(C):
                total = total + group[0, h, d, b] * group[1, h, d, b]
        stat = jnp.sum(total, axis=0, keepdims=True) / (NC * C * SC)
        old = diag[pl.ds(b, 1)]
        diag_out[pl.ds(b, 1)] = old - step_size * (stat - 1.0 / old)

    each(0, BLK, diag_step)
    for p in range(2):
        for h in range(NC):
            if p == 1:
                forwarded(p, h)
            copy = pltpu.make_async_copy(frecv[p][h], routed_out.at[p, h], local.at[2 + p * NC + h])
            copy.start()

    wait_all(score_z.at[pl.ds(1, Z - 1)], exch_s.at[0])
    wait_all(score_y.at[pl.ds(1, Y - 1)], exch_s.at[1])
    wait_all(score_c.at[pl.ds(1, C - 1)], exch_s.at[2])
    gather_sent(window_at, w_s, v_s)
    sent = Z // 2 * BLK - BLK // 2
    for p in range(2):
        for h in range(NC):
            for way in range(2):
                wait_all(field[p][h].at[pl.ds(0, sent)], ring_s.at[p, h, way])
            for i in range(Y - 1):
                wait_all(ysend[p][h].at[pl.ds(i * SLOTS, SLOTS)], y_s.at[p, h, i])
            wait_all(fsend[p][h].at[pl.ds(1, C - 1)], f_s.at[p, h])
    for h in range(NC):
        wait_all(psend[h].at[pl.ds(TD, (C - 1) * TD)], p_s.at[h])
        gather_sent(group_at(h), g_s.at[h], h_s.at[h])
    pltpu.make_async_copy(group, group_out, local.at[1]).wait()
    for p in range(2):
        for h in range(NC):
            pltpu.make_async_copy(
                frecv[p][h], routed_out.at[p, h], local.at[2 + p * NC + h]
            ).wait()


def step_kernel(info, routed, rows, tile, out):
    t = pl.program_id(0)
    samples = NC * C * SC
    flat = lambda ref, p: ref[p].reshape(samples, BS)
    left = jnp.concatenate([flat(rows, 1), flat(rows, 0)], axis=0)
    right = jnp.concatenate([flat(routed, 0), flat(routed, 1)], axis=0)
    left_hi, left_lo = split2(left)
    right_hi, right_lo = split2(right)
    dims = ((0,), (0,))
    total = dot(left_hi, right_hi, dims) + dot(left_hi, right_lo, dims) + dot(left_lo, right_hi, dims)
    stepped = tile[0] - (step_size * 0.5 / samples) * total
    i = lax.broadcasted_iota(jnp.int32, (BS, BS), 0)
    j = lax.broadcasted_iota(jnp.int32, (BS, BS), 1)
    flag = jnp.full((BS, BS), info[TD + t], jnp.int32)
    stepped = jnp.where((i == j) & (flag != 0), 0.0, stepped)
    limit = step_size * penalty
    out[0] = stepped - jnp.clip(stepped, -limit, limit)


def index_table(tile_rows, tile_cols, row, me):
    y, z = row // Z, row % Z
    groups = Y * Z
    tiles = C * TD
    wanted = ((y + jnp.arange(Y)) % Y) * Z + z
    take = wanted[:, None, None] == jnp.arange(groups)[None, :, None]
    cols = jnp.sum(jnp.where(take, tile_cols.reshape(1, groups, tiles), 0), axis=1)
    rows = jnp.sum(jnp.where(take[0], tile_rows.reshape(groups, tiles), 0), axis=0)
    source, local = cols // BLK, cols % BLK
    place = jnp.arange(tiles)
    rank = jnp.sum(
        (source[:, :, None] == source[:, None, :]) & (place[None, :] < place[:, None])[None],
        axis=2,
        dtype=jnp.int32,
    )
    slot = jnp.arange(SLOTS)
    chosen = (source[1:, None, :] == y * Z + slot[None, :, None] // CAP) & (
        rank[1:, None, :] == slot[None, :, None] % CAP
    )
    pick = jnp.sum(jnp.where(chosen, local[1:, None, :], 0), axis=2).reshape(-1)
    plane, depth = source[0] // Z, source[0] % Z
    away = (y - plane + Y) % Y
    fwd = jnp.where(
        away == 0,
        depth * BLK + local[0],
        PLANE + (away - 1) * SLOTS + depth * CAP + rank[0],
    )
    local_rows = rows - row * BLK
    before = (local_rows[None, :] < local_rows[:, None]) | (
        (local_rows[None, :] == local_rows[:, None]) & (place[None, :] < place[:, None])
    )
    position = jnp.sum(before, axis=1, dtype=jnp.int32)
    at = position[None, :] == place[:, None]
    lands = ((place // TD - me + C) % C) * TD + place % TD
    order = jnp.sum(jnp.where(at, lands[None, :], 0), axis=1)
    first = jnp.sum(local_rows[None, :] < local_rows[:, None], axis=1, dtype=jnp.int32)
    same = jnp.sum(jnp.where(at, (position > first)[None, :].astype(jnp.int32), 0), axis=1)
    blocks = jnp.arange(BLK)
    upto = jnp.sum(local_rows[None, :] <= blocks[:, None], axis=1, dtype=jnp.int32)
    count = jnp.sum(local_rows[None, :] == blocks[:, None], axis=1, dtype=jnp.int32)
    mine = (me * TD + jnp.arange(TD))[:, None] == place[None, :]
    my_rows = jnp.sum(jnp.where(mine, local_rows[None, :], 0), axis=1)
    on_diag = jnp.sum(jnp.where(mine, (rows == cols[0])[None, :].astype(jnp.int32), 0), axis=1)
    table = jnp.concatenate(
        [pick, fwd, order, same, jnp.maximum(upto - 1, 0), (count > 0).astype(jnp.int32), on_diag]
    )
    return table.astype(jnp.int32), jnp.concatenate([my_rows, on_diag]).astype(jnp.int32)


def per_device(samples, loadings, omega_tiles, omega_diagonal, tile_rows, tile_cols):
    row = lax.axis_index("rows")
    me = lax.axis_index("cols")
    factors = loadings.shape[0]
    ns = NC * SC
    table, info = index_table(tile_rows, tile_cols, row, me)
    f32 = jnp.float32
    vmem = lambda *shape: pltpu.VMEM(shape, f32)
    dma = lambda *shape: pltpu.SemaphoreType.DMA(shape)
    in_vmem = pl.BlockSpec(memory_space=pltpu.VMEM)
    anywhere = pl.BlockSpec(memory_space=pl.ANY)
    n = 2 * NC
    routed, group, new_diagonal = pl.pallas_call(
        route_kernel,
        out_shape=(
            jax.ShapeDtypeStruct((2, NC, C, TD, SC, BS), f32),
            jax.ShapeDtypeStruct((2, NC, C, BLK, SC, BS), f32),
            jax.ShapeDtypeStruct((BLK, BS), f32),
        ),
        in_specs=[
            pl.BlockSpec(memory_space=pltpu.SMEM),
            in_vmem,
            in_vmem,
            in_vmem,
            anywhere,
        ],
        out_specs=(anywhere, anywhere, in_vmem),
        scratch_shapes=[
            vmem(3, ns, factors),
            vmem(Z, ns, factors),
            vmem(Y, ns, factors),
            vmem(C, ns, factors),
            vmem(C, ns, BLK * BS),
            vmem(BLK, SC, BS),
            vmem(C * TD, SC, BS),
            vmem(TD, BS, BS),
            pltpu.VMEM((TD, BS, BS), jnp.bfloat16),
            pltpu.VMEM((TD, BS, BS), jnp.bfloat16),
            vmem(2, NC, C, BLK, SC, BS),
        ]
        + [vmem(PLANE + (Y - 1) * SLOTS, SC, BS)] * n
        + [vmem((Y - 1) * SLOTS, SC, BS)] * n
        + [vmem(C, TD, SC, BS)] * n
        + [vmem(C, TD, SC, BS)] * n
        + [vmem(C * TD, SC, BS)] * NC
        + [vmem(C * TD, SC, BS)] * NC
        + [
            dma(3),
            dma(3),
            dma(2, NC, 2),
            dma(2, NC, 2, Z // 2 + 1),
            dma(2, NC, Y - 1),
            dma(2, NC, Y - 1),
            dma(2, NC),
            dma(2, NC),
            dma(NC),
            dma(NC),
            dma(NC, C // 2),
            dma(NC, C // 2),
            dma(NC, C // 2),
            dma(NC, C // 2),
            dma(C // 2),
            dma(C // 2),
            dma(C // 2),
            dma(C // 2),
            dma(2 + n),
        ],
        compiler_params=pltpu.CompilerParams(
            collective_id=0, has_side_effects=True, vmem_limit_bytes=56 * 1024 * 1024
        ),
        name="route",
    )(table, samples, loadings, omega_diagonal.reshape(BLK, BS), omega_tiles)

    new_tiles = pl.pallas_call(
        step_kernel,
        out_shape=jax.ShapeDtypeStruct(omega_tiles.shape, f32),
        grid_spec=pltpu.PrefetchScalarGridSpec(
            num_scalar_prefetch=1,
            grid=(TD,),
            in_specs=[
                pl.BlockSpec((2, NC, C, None, SC, BS), lambda t, info: (0, 0, 0, t, 0, 0)),
                pl.BlockSpec((2, NC, C, None, SC, BS), lambda t, info: (0, 0, 0, info[t], 0, 0)),
                pl.BlockSpec((1, BS, BS), lambda t, info: (t, 0, 0)),
            ],
            out_specs=pl.BlockSpec((1, BS, BS), lambda t, info: (t, 0, 0)),
        ),
        compiler_params=pltpu.CompilerParams(vmem_limit_bytes=32 * 1024 * 1024),
        name="step",
    )(info, routed, group, omega_tiles)
    return new_tiles, new_diagonal.reshape(-1)


def solution(mesh):
    placed = (
        P("cols", "rows"),
        P(None, "rows"),
        P(("rows", "cols"), None, None),
        P("rows"),
        P(),
        P(),
    )
    return jax.shard_map(
        per_device,
        mesh=mesh,
        in_specs=placed,
        out_specs=(P(("rows", "cols"), None, None), P("rows")),
        check_vma=False,
    )
```

```python
import functools
import jax
import jax.numpy as jnp
from jax import lax
from jax.experimental import pallas as pl
from jax.experimental.pallas import tpu as pltpu
from jax.sharding import PartitionSpec as P

step_size = 0.5
penalty = 0.02
MESH = pl.DeviceIdType.MESH
CAP = 3
Y = 4
Z = 8
C = 8
BLK = 8
TD = 5
NC = 2
SC = 8
BS = 512
PLANE = Z * BLK
SLOTS = Z * CAP

PICK = 0
FWD = PICK + (Y - 1) * SLOTS
ORDER = FWD + C * TD
SAME = ORDER + C * TD
LAST = SAME + C * TD
HAS = LAST + BLK
DIAG = HAS + BLK
ROWS = DIAG + TD
META = ROWS + TD


def split2(x):
    hi = x.astype(jnp.bfloat16)
    return hi, (x - hi.astype(jnp.float32)).astype(jnp.bfloat16)


def split3(x):
    hi, rest = x.astype(jnp.bfloat16), None
    rest = x - hi.astype(jnp.float32)
    mid, low = split2(rest)
    return jnp.concatenate([hi, mid, low], axis=0)


def dot(a, b, dims):
    return lax.dot_general(a, b, (dims, ((), ())), preferred_element_type=jnp.float32)


def wait_all(ref, sem):
    pltpu.make_async_copy(ref, ref, sem).wait()


def route_kernel(
    meta,
    samples,
    loadings,
    diag,
    tiles,
    tiles_out,
    diag_out,
    part,
    score_z,
    score_y,
    score_c,
    window,
    stage,
    seg,
    tile_f32,
    tile_hi,
    tile_lo,
    *rest,
):
    n = 2 * NC
    pair = lambda flat: (flat[:NC], flat[NC:])
    field, ysend, fsend, frecv, group = (pair(rest[i * n : (i + 1) * n]) for i in range(5))
    rest = rest[5 * n :]
    psend, precv = rest[:NC], rest[NC : 2 * NC]
    (
        exch_s,
        exch_r,
        ring_s,
        ring_r,
        y_s,
        y_r,
        f_s,
        f_r,
        p_s,
        p_r,
        g_s,
        g_r,
        h_s,
        h_r,
        w_s,
        w_r,
        v_s,
        v_r,
        local,
    ) = rest[2 * NC :]

    row = lax.axis_index("rows")
    me = lax.axis_index("cols")
    y, z = row // Z, row % Z
    at_z = lambda d: {"rows": y * Z + (z + d + Z) % Z}
    at_y = lambda d: {"rows": ((y + d) % Y) * Z + z}
    at_c = lambda d: {"cols": (me + d + C) % C}
    side = 1 - 2 * (me % 2)
    other = at_c(side)

    def remote(src, dst, send, recv, where):
        return pltpu.make_async_remote_copy(
            src_ref=src,
            dst_ref=dst,
            send_sem=send,
            recv_sem=recv,
            device_id=where,
            device_id_type=MESH,
        )

    def each(low, high, body):
        lax.fori_loop(low, high, lambda i, _: (body(i), None)[1], None)

    barrier = pltpu.get_barrier_semaphore()

    def greet(where, count):
        each(
            1,
            count,
            lambda d: pl.semaphore_signal(
                barrier, inc=1, device_id=where(d), device_id_type=MESH
            ),
        )

    greet(at_z, Z)
    greet(at_y, Y)
    greet(at_c, C)
    tile_copy = pltpu.make_async_copy(tiles, tile_f32, local.at[0])
    tile_copy.start()

    def split_tiles(low, high):
        rows = lax.broadcasted_iota(jnp.int32, (BS // 4, BS), 0)
        cols = lax.broadcasted_iota(jnp.int32, (BS // 4, BS), 1)

        def one(i):
            t, q = i // 4, i % 4
            at = pl.ds(pl.multiple_of(q * (BS // 4), BS // 4), BS // 4)
            flag = jnp.full((BS // 4, BS), meta[DIAG + t], jnp.int32)
            drop = (rows + q * (BS // 4) == cols) & (flag != 0)
            hi, lo = split2(jnp.where(drop, 0.0, tile_f32[t, at]))
            tile_hi[t, at] = hi
            tile_lo[t, at] = lo

        each(low, high, one)

    def score_step(b, total):
        cols = pl.ds(pl.multiple_of(b * BS, BS), BS)
        return total + dot(split3(samples[:, cols]), loadings[:, cols], ((1,), (1,)))

    ns = NC * SC
    total = lax.fori_loop(0, BLK, score_step, jnp.zeros((3 * ns, loadings.shape[0]), jnp.float32))
    part[0] = total[:ns] + total[ns : 2 * ns] + total[2 * ns :]
    pl.semaphore_wait(barrier, Z + Y + C - 3)

    def gather_start(src, place, far_s, far_r, near_s, near_r):
        each(
            1,
            C // 2,
            lambda q: remote(src, place(2 * q), far_s.at[q], far_r.at[q], at_c(2 * q)).start(),
        )
        remote(src, place((side + C) % C), near_s.at[0], near_r.at[0], other).start()

    def gather_pass(place, far_r, near_s, near_r):
        def one(q):
            wait_all(place(2 * q), far_r.at[q])
            remote(
                place(2 * q), place((side + 2 * q + C) % C), near_s.at[q], near_r.at[q], other
            ).start()

        each(1, C // 2, one)

    def gathered(place, near_r):
        each(0, C // 2, lambda q: wait_all(place((2 * q - side + C) % C), near_r.at[q]))

    def gather_sent(place, far_s, near_s):
        each(1, C // 2, lambda q: wait_all(place(2 * q), far_s.at[q]))
        each(0, C // 2, lambda q: wait_all(place(2 * q), near_s.at[q]))

    window_at = lambda d: window.at[d]

    each(
        1,
        Z,
        lambda d: remote(part.at[0], score_z.at[d], exch_s.at[0], exch_r.at[0], at_z(d)).start(),
    )
    gather_start(samples, window_at, w_s, w_r, v_s, v_r)
    tile_copy.wait()
    split_tiles(0, 12)
    wait_all(score_z.at[pl.ds(1, Z - 1)], exch_r.at[0])
    total = part[0]
    for d in range(1, Z):
        total = total + score_z[d]
    part[1] = total
    each(
        1,
        Y,
        lambda d: remote(part.at[1], score_y.at[d], exch_s.at[1], exch_r.at[1], at_y(d)).start(),
    )
    split_tiles(12, TD * 4)
    wait_all(score_y.at[pl.ds(1, Y - 1)], exch_r.at[1])
    for d in range(1, Y):
        total = total + score_y[d]
    scores = split3(total)
    part[2] = total

    def residual_step(b):
        cols = pl.ds(pl.multiple_of(b * BS, BS), BS)
        terms = dot(scores, loadings[:, cols], ((1,), (0,)))
        value = samples[:, cols] - (terms[:ns] + terms[ns : 2 * ns] + terms[2 * ns :])
        for h in range(NC):
            field[0][h][z * BLK + b] = value[h * SC : (h + 1) * SC]
            group[0][h][0, b] = value[h * SC : (h + 1) * SC]

    each(0, BLK, residual_step)

    def group_residual():
        gathered(window_at, v_r)
        wait_all(score_c.at[pl.ds(1, C - 1)], exch_r.at[2])
        far = (C - 1) * ns
        terms3 = split3(score_c[1:].reshape(far, loadings.shape[0]))

        def one(b):
            cols = pl.ds(pl.multiple_of(b * BS, BS), BS)
            terms = dot(terms3, loadings[:, cols], ((1,), (0,)))
            terms = terms[:far] + terms[far : 2 * far] + terms[2 * far :]
            value = window[pl.ds(1, C - 1), :, cols] - terms.reshape(C - 1, ns, BS)
            for h in range(NC):
                group[0][h][pl.ds(1, C - 1), b] = value[:, h * SC : (h + 1) * SC]

        each(0, BLK, one)

    half = BLK // 2

    def hop(p, h, k, u, right):
        slice_of = ((z - k + 1 + Z) if right else (z + k - 1)) % Z
        ref = field[p][h].at[pl.ds(slice_of * BLK + u * half, half)]
        way = 0 if right else 1
        return remote(
            ref,
            ref,
            ring_s.at[p, h, way],
            ring_r.at[p, h, way, k, u],
            at_z(1 if right else -1),
        )

    def arrived(p, h, k, u, right):
        slice_of = ((z - k + Z) if right else (z + k)) % Z
        ref = field[p][h].at[pl.ds(slice_of * BLK + u * half, half)]
        wait_all(ref, ring_r.at[p, h, 0 if right else 1, k, u])

    def send_picks(p, h, zs):
        ref = field[p][h]
        stage[...] = ref[pl.ds(zs * BLK, BLK)]

        def to_plane(i):
            base = i * SLOTS + zs * CAP
            for j in range(CAP):
                ysend[p][h][base + j] = stage[meta[PICK + base + j]]
            remote(
                ysend[p][h].at[pl.ds(base, CAP)],
                ref.at[pl.ds(PLANE + base, CAP)],
                y_s.at[p, h, i],
                y_r.at[p, h, i],
                at_y(i + 1),
            ).start()

        each(0, Y - 1, to_plane)

    def ring_start(p, h):
        for u in range(2):
            hop(p, h, 1, u, True).start()
            hop(p, h, 1, 1 - u, False).start()

    def ring_step(p, h, k, last=False):
        for u in range(2):
            arrived(p, h, k, u, True)
            if not last or u == 0:
                hop(p, h, k + 1, u, True).start()
            arrived(p, h, k, 1 - u, False)
            if not last or u == 0:
                hop(p, h, k + 1, 1 - u, False).start()
        picks_at(p, h, k)

    def ring_end(p, h):
        arrived(p, h, Z // 2, 0, True)
        arrived(p, h, Z // 2, 1, False)
        send_picks(p, h, (z + Z // 2) % Z)

    def picks_at(p, h, k):
        send_picks(p, h, (z - k + Z) % Z)
        send_picks(p, h, (z + k) % Z)

    def routed(p, h):
        for i in range(Y - 1):
            wait_all(field[p][h].at[pl.ds(PLANE + i * SLOTS, SLOTS)], y_r.at[p, h, i])

    def forward(p, h):
        def tile(t):
            def one(d):
                dest = (me + d) % C
                at = d * TD + t
                fsend[p][h][at] = field[p][h][meta[FWD + dest * TD + t]]
                remote(
                    fsend[p][h].at[at],
                    frecv[p][h].at[t, d],
                    f_s.at[p, h],
                    f_r.at[p, h, t],
                    at_c(d),
                ).start()

            each(1, C, one)
            frecv[p][h][t, 0] = field[p][h][meta[FWD + me * TD + t]]

        each(0, TD, tile)

    def forwarded(p, h, t):
        wait_all(frecv[p][h].at[t, pl.ds(1, C - 1)], f_r.at[p, h, t])

    def products(h):
        def one(t):
            forwarded(0, h, t)
            hi, lo = split2(frecv[0][h][t].reshape(C * SC, BS))
            both = dot(jnp.concatenate([hi, lo], axis=0), tile_hi[t], ((1,), (1,)))
            value = both[: C * SC] + both[C * SC :] + dot(hi, tile_lo[t], ((1,), (1,)))
            value = value.reshape(C, SC, BS)
            precv[h][t] = value[0]
            for d in range(1, C):
                psend[h][d * TD + t] = value[d]
            each(
                1,
                C,
                lambda d: remote(
                    psend[h].at[d * TD + t],
                    precv[h].at[d * TD + t],
                    p_s.at[h],
                    p_r.at[h],
                    at_c(-d),
                ).start(),
            )

        each(0, TD, one)

    def apply_rows(h):
        wait_all(precv[h].at[pl.ds(TD, (C - 1) * TD)], p_r.at[h])

        def one(k, running):
            same = jnp.full((SC, BS), meta[SAME + k], jnp.int32) != 0
            running = jnp.where(same, running, 0.0) + precv[h][meta[ORDER + k]]
            seg[k] = running
            return running

        lax.fori_loop(0, C * TD, one, jnp.zeros((SC, BS), jnp.float32))

        def block(b):
            has = jnp.full((SC, BS), meta[HAS + b], jnp.int32) != 0
            value = jnp.where(has, seg[meta[LAST + b]], 0.0)
            value = value + diag[pl.ds(b, 1)] * group[0][h][0, b]
            field[1][h][z * BLK + b] = value
            group[1][h][0, b] = value

        each(0, BLK, block)

    group_at = lambda h: lambda d: group[1][h].at[d]

    def rows_start(h):
        gather_start(group[1][h].at[0], group_at(h), g_s.at[h], g_r.at[h], h_s.at[h], h_r.at[h])

    def rows_pass(h):
        gather_pass(group_at(h), g_r.at[h], h_s.at[h], h_r.at[h])

    scale = step_size * 0.5 / (NC * C * SC)

    def gradient_step(h, finish):
        def one(t):
            forwarded(1, h, t)
            block = meta[ROWS + t]
            rows = lambda p: group[p][h][:, block].reshape(C * SC, BS)
            left_hi, left_lo = split2(jnp.concatenate([rows(1), rows(0)], axis=0))
            right = [frecv[p][h][t].reshape(C * SC, BS) for p in range(2)]
            right_hi, right_lo = split2(jnp.concatenate(right, axis=0))
            left = jnp.concatenate([left_hi, left_hi, left_lo], axis=0)
            right = jnp.concatenate([right_hi, right_lo, right_hi], axis=0)
            total = dot(left, right, ((0,), (0,)))
            stepped = tile_f32[t] - scale * total
            if finish:
                i = lax.broadcasted_iota(jnp.int32, (BS, BS), 0)
                j = lax.broadcasted_iota(jnp.int32, (BS, BS), 1)
                flag = jnp.full((BS, BS), meta[DIAG + t], jnp.int32)
                stepped = jnp.where((i == j) & (flag != 0), 0.0, stepped)
                limit = step_size * penalty
                stepped = stepped - jnp.clip(stepped, -limit, limit)
            tile_f32[t] = stepped
            if finish:
                pltpu.make_async_copy(tile_f32.at[t], tiles_out.at[t], local.at[1 + t]).start()

        each(0, TD, one)

    def diag_step(b):
        total = jnp.zeros((SC, BS), jnp.float32)
        for h in range(NC):
            for d in range(C):
                total = total + group[0][h][d, b] * group[1][h][d, b]
        stat = jnp.sum(total, axis=0, keepdims=True) / (NC * C * SC)
        old = diag[pl.ds(b, 1)]
        diag_out[pl.ds(b, 1)] = old - step_size * (stat - 1.0 / old)

    far_step = Z // 2 - 1

    ring_start(0, 0)
    send_picks(0, 0, z)
    send_picks(0, 1, z)
    each(
        1,
        C,
        lambda d: remote(part.at[2], score_c.at[d], exch_s.at[2], exch_r.at[2], at_c(d)).start(),
    )
    each(1, far_step, lambda k: ring_step(0, 0, k))
    ring_step(0, 0, far_step, last=True)
    ring_start(0, 1)
    gather_pass(window_at, w_r, v_s, v_r)
    ring_end(0, 0)
    each(1, far_step, lambda k: ring_step(0, 1, k))
    routed(0, 0)
    forward(0, 0)
    ring_step(0, 1, far_step, last=True)
    ring_end(0, 1)
    products(0)
    group_residual()
    routed(0, 1)
    forward(0, 1)

    apply_rows(0)
    ring_start(1, 0)
    send_picks(1, 0, z)
    rows_start(0)
    each(1, far_step, lambda k: ring_step(1, 0, k))
    ring_step(1, 0, far_step, last=True)
    products(1)
    ring_end(1, 0)
    rows_pass(0)

    apply_rows(1)
    ring_start(1, 1)
    send_picks(1, 1, z)
    routed(1, 0)
    forward(1, 0)
    rows_start(1)
    each(1, far_step, lambda k: ring_step(1, 1, k))
    ring_step(1, 1, far_step, last=True)
    ring_end(1, 1)
    rows_pass(1)
    gathered(group_at(0), h_r.at[0])
    gradient_step(0, False)
    gathered(group_at(1), h_r.at[1])
    each(0, BLK, diag_step)
    routed(1, 1)
    forward(1, 1)
    gradient_step(1, True)

    wait_all(score_z.at[pl.ds(1, Z - 1)], exch_s.at[0])
    wait_all(score_y.at[pl.ds(1, Y - 1)], exch_s.at[1])
    wait_all(score_c.at[pl.ds(1, C - 1)], exch_s.at[2])
    gather_sent(window_at, w_s, v_s)
    sent = Z // 2 * BLK - BLK // 2
    for p in range(2):
        for h in range(NC):
            for way in range(2):
                wait_all(field[p][h].at[pl.ds(0, sent)], ring_s.at[p, h, way])
            for i in range(Y - 1):
                wait_all(ysend[p][h].at[pl.ds(i * SLOTS, SLOTS)], y_s.at[p, h, i])
            wait_all(fsend[p][h].at[pl.ds(TD, (C - 1) * TD)], f_s.at[p, h])
    for h in range(NC):
        wait_all(psend[h].at[pl.ds(TD, (C - 1) * TD)], p_s.at[h])
        gather_sent(group_at(h), g_s.at[h], h_s.at[h])
    for t in range(TD):
        pltpu.make_async_copy(tile_f32.at[t], tiles_out.at[t], local.at[1 + t]).wait()


def index_table(tile_rows, tile_cols, row, me):
    y, z = row // Z, row % Z
    groups = Y * Z
    tiles = C * TD
    wanted = ((y + jnp.arange(Y)) % Y) * Z + z
    take = wanted[:, None, None] == jnp.arange(groups)[None, :, None]
    cols = jnp.sum(jnp.where(take, tile_cols.reshape(1, groups, tiles), 0), axis=1)
    rows = jnp.sum(jnp.where(take[0], tile_rows.reshape(groups, tiles), 0), axis=0)
    source, local = cols // BLK, cols % BLK
    place = jnp.arange(tiles)
    rank = jnp.sum(
        (source[:, :, None] == source[:, None, :]) & (place[None, :] < place[:, None])[None],
        axis=2,
        dtype=jnp.int32,
    )
    slot = jnp.arange(SLOTS)
    chosen = (source[1:, None, :] == y * Z + slot[None, :, None] // CAP) & (
        rank[1:, None, :] == slot[None, :, None] % CAP
    )
    pick = jnp.sum(jnp.where(chosen, local[1:, None, :], 0), axis=2).reshape(-1)
    plane, depth = source[0] // Z, source[0] % Z
    away = (y - plane + Y) % Y
    fwd = jnp.where(
        away == 0,
        depth * BLK + local[0],
        PLANE + (away - 1) * SLOTS + depth * CAP + rank[0],
    )
    local_rows = rows - row * BLK
    before = (local_rows[None, :] < local_rows[:, None]) | (
        (local_rows[None, :] == local_rows[:, None]) & (place[None, :] < place[:, None])
    )
    position = jnp.sum(before, axis=1, dtype=jnp.int32)
    at = position[None, :] == place[:, None]
    lands = ((place // TD - me + C) % C) * TD + place % TD
    order = jnp.sum(jnp.where(at, lands[None, :], 0), axis=1)
    first = jnp.sum(local_rows[None, :] < local_rows[:, None], axis=1, dtype=jnp.int32)
    same = jnp.sum(jnp.where(at, (position > first)[None, :].astype(jnp.int32), 0), axis=1)
    blocks = jnp.arange(BLK)
    upto = jnp.sum(local_rows[None, :] <= blocks[:, None], axis=1, dtype=jnp.int32)
    count = jnp.sum(local_rows[None, :] == blocks[:, None], axis=1, dtype=jnp.int32)
    mine = (me * TD + jnp.arange(TD))[:, None] == place[None, :]
    my_rows = jnp.sum(jnp.where(mine, local_rows[None, :], 0), axis=1)
    on_diag = jnp.sum(jnp.where(mine, (rows == cols[0])[None, :].astype(jnp.int32), 0), axis=1)
    table = jnp.concatenate(
        [pick, fwd, order, same, jnp.maximum(upto - 1, 0), (count > 0).astype(jnp.int32), on_diag, my_rows]
    )
    return table.astype(jnp.int32)


def per_device(samples, loadings, omega_tiles, omega_diagonal, tile_rows, tile_cols):
    row = lax.axis_index("rows")
    me = lax.axis_index("cols")
    factors = loadings.shape[0]
    ns = NC * SC
    table = index_table(tile_rows, tile_cols, row, me)
    f32 = jnp.float32
    vmem = lambda *shape: pltpu.VMEM(shape, f32)
    dma = lambda *shape: pltpu.SemaphoreType.DMA(shape)
    in_vmem = pl.BlockSpec(memory_space=pltpu.VMEM)
    anywhere = pl.BlockSpec(memory_space=pl.ANY)
    n = 2 * NC
    new_tiles, new_diagonal = pl.pallas_call(
        route_kernel,
        out_shape=(
            jax.ShapeDtypeStruct(omega_tiles.shape, f32),
            jax.ShapeDtypeStruct((BLK, BS), f32),
        ),
        in_specs=[
            pl.BlockSpec(memory_space=pltpu.SMEM),
            in_vmem,
            in_vmem,
            in_vmem,
            anywhere,
        ],
        out_specs=(anywhere, in_vmem),
        scratch_shapes=[
            vmem(3, ns, factors),
            vmem(Z, ns, factors),
            vmem(Y, ns, factors),
            vmem(C, ns, factors),
            vmem(C, ns, BLK * BS),
            vmem(BLK, SC, BS),
            vmem(C * TD, SC, BS),
            vmem(TD, BS, BS),
            pltpu.VMEM((TD, BS, BS), jnp.bfloat16),
            pltpu.VMEM((TD, BS, BS), jnp.bfloat16),
        ]
        + [vmem(PLANE + (Y - 1) * SLOTS, SC, BS)] * n
        + [vmem((Y - 1) * SLOTS, SC, BS)] * n
        + [vmem(C * TD, SC, BS)] * n
        + [vmem(TD, C, SC, BS)] * n
        + [vmem(C, BLK, SC, BS)] * n
        + [vmem(C * TD, SC, BS)] * NC
        + [vmem(C * TD, SC, BS)] * NC
        + [
            dma(3),
            dma(3),
            dma(2, NC, 2),
            dma(2, NC, 2, Z // 2 + 1, 2),
            dma(2, NC, Y - 1),
            dma(2, NC, Y - 1),
            dma(2, NC),
            dma(2, NC, TD),
            dma(NC),
            dma(NC),
            dma(NC, C // 2),
            dma(NC, C // 2),
            dma(NC, C // 2),
            dma(NC, C // 2),
            dma(C // 2),
            dma(C // 2),
            dma(C // 2),
            dma(C // 2),
            dma(1 + TD),
        ],
        compiler_params=pltpu.CompilerParams(
            collective_id=0, has_side_effects=True, vmem_limit_bytes=56 * 1024 * 1024
        ),
        name="route",
    )(table, samples, loadings, omega_diagonal.reshape(BLK, BS), omega_tiles)

    return new_tiles, new_diagonal.reshape(-1)


def solution(mesh):
    placed = (
        P("cols", "rows"),
        P(None, "rows"),
        P(("rows", "cols"), None, None),
        P("rows"),
        P(),
        P(),
    )
    return jax.shard_map(
        per_device,
        mesh=mesh,
        in_specs=placed,
        out_specs=(P(("rows", "cols"), None, None), P("rows")),
        check_vma=False,
    )
```

```python
import functools
import jax
import jax.numpy as jnp
from jax import lax
from jax.experimental import pallas as pl
from jax.experimental.pallas import tpu as pltpu
from jax.sharding import PartitionSpec as P

step_size = 0.5
penalty = 0.02
MESH = pl.DeviceIdType.MESH
CAP = 3
Y = 4
Z = 8
C = 8
BLK = 8
TD = 5
NC = 2
SC = 8
BS = 512
PLANE = Z * BLK
SLOTS = Z * CAP

PICK = 0
FWD = PICK + (Y - 1) * SLOTS
ORDER = FWD + C * TD
SAME = ORDER + C * TD
LAST = SAME + C * TD
HAS = LAST + BLK
DIAG = HAS + BLK
ROWS = DIAG + TD
META = ROWS + TD


def split2(x):
    hi = x.astype(jnp.bfloat16)
    return hi, (x - hi.astype(jnp.float32)).astype(jnp.bfloat16)


def split3(x):
    hi, rest = x.astype(jnp.bfloat16), None
    rest = x - hi.astype(jnp.float32)
    mid, low = split2(rest)
    return jnp.concatenate([hi, mid, low], axis=0)


def dot(a, b, dims):
    return lax.dot_general(a, b, (dims, ((), ())), preferred_element_type=jnp.float32)


def wait_all(ref, sem):
    pltpu.make_async_copy(ref, ref, sem).wait()


def route_kernel(
    meta,
    samples,
    loadings,
    diag,
    tiles,
    tiles_out,
    diag_out,
    part,
    score_z,
    score_y,
    score_c,
    window,
    stage,
    seg,
    tile_f32,
    tile_hi,
    tile_lo,
    *rest,
):
    n = 2 * NC
    pair = lambda flat: (flat[:NC], flat[NC:])
    field, ysend, fsend, frecv, group = (pair(rest[i * n : (i + 1) * n]) for i in range(5))
    rest = rest[5 * n :]
    psend, precv = rest[:NC], rest[NC : 2 * NC]
    (
        exch_s,
        exch_r,
        ring_s,
        ring_r,
        y_s,
        y_r,
        f_s,
        f_r,
        p_s,
        p_r,
        g_s,
        g_r,
        h_s,
        h_r,
        w_s,
        w_r,
        v_s,
        v_r,
        local,
    ) = rest[2 * NC :]

    row = lax.axis_index("rows")
    me = lax.axis_index("cols")
    y, z = row // Z, row % Z
    at_z = lambda d: {"rows": y * Z + (z + d + Z) % Z}
    at_y = lambda d: {"rows": ((y + d) % Y) * Z + z}
    at_c = lambda d: {"cols": (me + d + C) % C}
    side = 1 - 2 * (me % 2)
    other = at_c(side)

    def remote(src, dst, send, recv, where):
        return pltpu.make_async_remote_copy(
            src_ref=src,
            dst_ref=dst,
            send_sem=send,
            recv_sem=recv,
            device_id=where,
            device_id_type=MESH,
        )

    def each(low, high, body):
        lax.fori_loop(low, high, lambda i, _: (body(i), None)[1], None)

    barrier = pltpu.get_barrier_semaphore()

    def greet(where, count):
        each(
            1,
            count,
            lambda d: pl.semaphore_signal(
                barrier, inc=1, device_id=where(d), device_id_type=MESH
            ),
        )

    greet(at_z, Z)
    greet(at_y, Y)
    greet(at_c, C)
    tile_copy = pltpu.make_async_copy(tiles, tile_f32, local.at[0])
    tile_copy.start()

    def split_tiles(low, high):
        rows = lax.broadcasted_iota(jnp.int32, (BS // 4, BS), 0)
        cols = lax.broadcasted_iota(jnp.int32, (BS // 4, BS), 1)

        def one(i):
            t, q = i // 4, i % 4
            at = pl.ds(pl.multiple_of(q * (BS // 4), BS // 4), BS // 4)
            flag = jnp.full((BS // 4, BS), meta[DIAG + t], jnp.int32)
            drop = (rows + q * (BS // 4) == cols) & (flag != 0)
            hi, lo = split2(jnp.where(drop, 0.0, tile_f32[t, at]))
            tile_hi[t, at] = hi
            tile_lo[t, at] = lo

        each(low, high, one)

    def score_step(b, total):
        cols = pl.ds(pl.multiple_of(b * BS, BS), BS)
        return total + dot(split3(samples[:, cols]), loadings[:, cols], ((1,), (1,)))

    ns = NC * SC
    total = lax.fori_loop(0, BLK, score_step, jnp.zeros((3 * ns, loadings.shape[0]), jnp.float32))
    part[0] = total[:ns] + total[ns : 2 * ns] + total[2 * ns :]
    pl.semaphore_wait(barrier, Z + Y + C - 3)

    def gather_start(src, place, far_s, far_r, near_s, near_r):
        each(
            1,
            C // 2,
            lambda q: remote(src, place(2 * q), far_s.at[q], far_r.at[q], at_c(2 * q)).start(),
        )
        remote(src, place((side + C) % C), near_s.at[0], near_r.at[0], other).start()

    def gather_pass(place, far_r, near_s, near_r):
        def one(q):
            wait_all(place(2 * q), far_r.at[q])
            remote(
                place(2 * q), place((side + 2 * q + C) % C), near_s.at[q], near_r.at[q], other
            ).start()

        each(1, C // 2, one)

    def gathered(place, near_r):
        each(0, C // 2, lambda q: wait_all(place((2 * q - side + C) % C), near_r.at[q]))

    def gather_sent(place, far_s, near_s):
        each(1, C // 2, lambda q: wait_all(place(2 * q), far_s.at[q]))
        each(0, C // 2, lambda q: wait_all(place(2 * q), near_s.at[q]))

    window_at = lambda d: window.at[d]

    each(
        1,
        Z,
        lambda d: remote(part.at[0], score_z.at[d], exch_s.at[0], exch_r.at[0], at_z(d)).start(),
    )
    gather_start(samples, window_at, w_s, w_r, v_s, v_r)
    tile_copy.wait()
    split_tiles(0, 12)
    wait_all(score_z.at[pl.ds(1, Z - 1)], exch_r.at[0])
    total = part[0]
    for d in range(1, Z):
        total = total + score_z[d]
    part[1] = total
    each(
        1,
        Y,
        lambda d: remote(part.at[1], score_y.at[d], exch_s.at[1], exch_r.at[1], at_y(d)).start(),
    )
    split_tiles(12, TD * 4)
    wait_all(score_y.at[pl.ds(1, Y - 1)], exch_r.at[1])
    for d in range(1, Y):
        total = total + score_y[d]
    scores = split3(total)
    part[2] = total

    def residual_step(b):
        cols = pl.ds(pl.multiple_of(b * BS, BS), BS)
        terms = dot(scores, loadings[:, cols], ((1,), (0,)))
        value = samples[:, cols] - (terms[:ns] + terms[ns : 2 * ns] + terms[2 * ns :])
        for h in range(NC):
            field[0][h][z * BLK + b] = value[h * SC : (h + 1) * SC]
            group[0][h][0, b] = value[h * SC : (h + 1) * SC]

    each(0, BLK, residual_step)

    def group_residual():
        gathered(window_at, v_r)
        wait_all(score_c.at[pl.ds(1, C - 1)], exch_r.at[2])
        far = (C - 1) * ns
        terms3 = split3(score_c[1:].reshape(far, loadings.shape[0]))

        def one(b):
            cols = pl.ds(pl.multiple_of(b * BS, BS), BS)
            terms = dot(terms3, loadings[:, cols], ((1,), (0,)))
            terms = terms[:far] + terms[far : 2 * far] + terms[2 * far :]
            value = window[pl.ds(1, C - 1), :, cols] - terms.reshape(C - 1, ns, BS)
            for h in range(NC):
                group[0][h][pl.ds(1, C - 1), b] = value[:, h * SC : (h + 1) * SC]

        each(0, BLK, one)

    half = BLK // 2

    def hop(p, h, k, u, right):
        slice_of = ((z - k + 1 + Z) if right else (z + k - 1)) % Z
        ref = field[p][h].at[pl.ds(slice_of * BLK + u * half, half)]
        way = 0 if right else 1
        return remote(
            ref,
            ref,
            ring_s.at[p, h, way],
            ring_r.at[p, h, way, k, u],
            at_z(1 if right else -1),
        )

    def arrived(p, h, k, u, right):
        slice_of = ((z - k + Z) if right else (z + k)) % Z
        ref = field[p][h].at[pl.ds(slice_of * BLK + u * half, half)]
        wait_all(ref, ring_r.at[p, h, 0 if right else 1, k, u])

    def send_picks(p, h, zs):
        ref = field[p][h]
        stage[...] = ref[pl.ds(zs * BLK, BLK)]

        def to_plane(i):
            base = i * SLOTS + zs * CAP
            for j in range(CAP):
                ysend[p][h][base + j] = stage[meta[PICK + base + j]]
            remote(
                ysend[p][h].at[pl.ds(base, CAP)],
                ref.at[pl.ds(PLANE + base, CAP)],
                y_s.at[p, h, i],
                y_r.at[p, h, i],
                at_y(i + 1),
            ).start()

        each(0, Y - 1, to_plane)

    def ring_start(p, h):
        for u in range(2):
            hop(p, h, 1, u, True).start()
            hop(p, h, 1, 1 - u, False).start()

    def ring_step(p, h, k, last=False):
        for u in range(2):
            arrived(p, h, k, u, True)
            if not last or u == 0:
                hop(p, h, k + 1, u, True).start()
            arrived(p, h, k, 1 - u, False)
            if not last or u == 0:
                hop(p, h, k + 1, 1 - u, False).start()
        picks_at(p, h, k)

    def ring_end(p, h):
        arrived(p, h, Z // 2, 0, True)
        arrived(p, h, Z // 2, 1, False)
        send_picks(p, h, (z + Z // 2) % Z)

    def picks_at(p, h, k):
        send_picks(p, h, (z - k + Z) % Z)
        send_picks(p, h, (z + k) % Z)

    def routed(p, h):
        for i in range(Y - 1):
            wait_all(field[p][h].at[pl.ds(PLANE + i * SLOTS, SLOTS)], y_r.at[p, h, i])

    def forward(p, h):
        def tile(t):
            def one(d):
                dest = (me + d) % C
                at = d * TD + t
                fsend[p][h][at] = field[p][h][meta[FWD + dest * TD + t]]
                remote(
                    fsend[p][h].at[at],
                    frecv[p][h].at[t, d],
                    f_s.at[p, h],
                    f_r.at[p, h, t],
                    at_c(d),
                ).start()

            each(1, C, one)
            frecv[p][h][t, 0] = field[p][h][meta[FWD + me * TD + t]]

        each(0, TD, tile)

    def forwarded(p, h, t):
        wait_all(frecv[p][h].at[t, pl.ds(1, C - 1)], f_r.at[p, h, t])

    def products(h):
        def one(t):
            forwarded(0, h, t)
            hi, lo = split2(frecv[0][h][t].reshape(C * SC, BS))
            both = dot(jnp.concatenate([hi, lo], axis=0), tile_hi[t], ((1,), (1,)))
            value = both[: C * SC] + both[C * SC :] + dot(hi, tile_lo[t], ((1,), (1,)))
            value = value.reshape(C, SC, BS)
            precv[h][t] = value[0]
            for d in range(1, C):
                psend[h][d * TD + t] = value[d]
            each(
                1,
                C,
                lambda d: remote(
                    psend[h].at[d * TD + t],
                    precv[h].at[d * TD + t],
                    p_s.at[h],
                    p_r.at[h],
                    at_c(-d),
                ).start(),
            )

        each(0, TD, one)

    def apply_rows(h):
        wait_all(precv[h].at[pl.ds(TD, (C - 1) * TD)], p_r.at[h])

        def one(k, running):
            same = jnp.full((SC, BS), meta[SAME + k], jnp.int32) != 0
            running = jnp.where(same, running, 0.0) + precv[h][meta[ORDER + k]]
            seg[k] = running
            return running

        lax.fori_loop(0, C * TD, one, jnp.zeros((SC, BS), jnp.float32))

        def block(b):
            has = jnp.full((SC, BS), meta[HAS + b], jnp.int32) != 0
            value = jnp.where(has, seg[meta[LAST + b]], 0.0)
            value = value + diag[:, pl.ds(pl.multiple_of(b * BS, BS), BS)] * group[0][h][0, b]
            field[1][h][z * BLK + b] = value
            group[1][h][0, b] = value

        each(0, BLK, block)

    group_at = lambda h: lambda d: group[1][h].at[d]

    def rows_start(h):
        gather_start(group[1][h].at[0], group_at(h), g_s.at[h], g_r.at[h], h_s.at[h], h_r.at[h])

    def rows_pass(h):
        gather_pass(group_at(h), g_r.at[h], h_s.at[h], h_r.at[h])

    scale = step_size * 0.5 / (NC * C * SC)

    def gradient_step(h, finish):
        def one(t):
            forwarded(1, h, t)
            block = meta[ROWS + t]
            rows = lambda p: group[p][h][:, block].reshape(C * SC, BS)
            left_hi, left_lo = split2(jnp.concatenate([rows(1), rows(0)], axis=0))
            right = [frecv[p][h][t].reshape(C * SC, BS) for p in range(2)]
            right_hi, right_lo = split2(jnp.concatenate(right, axis=0))
            left = jnp.concatenate([left_hi, left_hi, left_lo], axis=0)
            right = jnp.concatenate([right_hi, right_lo, right_hi], axis=0)
            total = dot(left, right, ((0,), (0,)))
            stepped = tile_f32[t] - scale * total
            if finish:
                i = lax.broadcasted_iota(jnp.int32, (BS, BS), 0)
                j = lax.broadcasted_iota(jnp.int32, (BS, BS), 1)
                flag = jnp.full((BS, BS), meta[DIAG + t], jnp.int32)
                stepped = jnp.where((i == j) & (flag != 0), 0.0, stepped)
            tile_f32[t] = stepped
            if finish:
                pltpu.make_async_copy(tile_f32.at[t], tiles_out.at[t], local.at[1 + t]).start()

        each(0, TD, one)

    def diag_step(b):
        total = jnp.zeros((SC, BS), jnp.float32)
        for h in range(NC):
            for d in range(C):
                total = total + group[0][h][d, b] * group[1][h][d, b]
        stat = jnp.sum(total, axis=0, keepdims=True) / (NC * C * SC)
        at = pl.ds(pl.multiple_of(b * BS, BS), BS)
        old = diag[:, at]
        diag_out[:, at] = old - step_size * (stat - 1.0 / old)

    far_step = Z // 2 - 1

    ring_start(0, 0)
    send_picks(0, 0, z)
    send_picks(0, 1, z)
    each(
        1,
        C,
        lambda d: remote(part.at[2], score_c.at[d], exch_s.at[2], exch_r.at[2], at_c(d)).start(),
    )
    each(1, far_step, lambda k: ring_step(0, 0, k))
    ring_step(0, 0, far_step, last=True)
    ring_start(0, 1)
    gather_pass(window_at, w_r, v_s, v_r)
    ring_end(0, 0)
    each(1, far_step, lambda k: ring_step(0, 1, k))
    routed(0, 0)
    forward(0, 0)
    ring_step(0, 1, far_step, last=True)
    ring_end(0, 1)
    products(0)
    group_residual()

    apply_rows(0)
    ring_start(1, 0)
    send_picks(1, 0, z)
    routed(0, 1)
    forward(0, 1)
    rows_start(0)
    each(1, far_step, lambda k: ring_step(1, 0, k))
    ring_step(1, 0, far_step, last=True)
    products(1)
    ring_end(1, 0)
    rows_pass(0)

    apply_rows(1)
    ring_start(1, 1)
    send_picks(1, 1, z)
    routed(1, 0)
    forward(1, 0)
    rows_start(1)
    each(1, far_step, lambda k: ring_step(1, 1, k))
    ring_step(1, 1, far_step, last=True)
    ring_end(1, 1)
    rows_pass(1)
    gathered(group_at(0), h_r.at[0])
    gradient_step(0, False)
    gathered(group_at(1), h_r.at[1])
    each(0, BLK, diag_step)
    routed(1, 1)
    forward(1, 1)
    gradient_step(1, True)

    wait_all(score_z.at[pl.ds(1, Z - 1)], exch_s.at[0])
    wait_all(score_y.at[pl.ds(1, Y - 1)], exch_s.at[1])
    wait_all(score_c.at[pl.ds(1, C - 1)], exch_s.at[2])
    gather_sent(window_at, w_s, v_s)
    sent = Z // 2 * BLK - BLK // 2
    for p in range(2):
        for h in range(NC):
            for way in range(2):
                wait_all(field[p][h].at[pl.ds(0, sent)], ring_s.at[p, h, way])
            for i in range(Y - 1):
                wait_all(ysend[p][h].at[pl.ds(i * SLOTS, SLOTS)], y_s.at[p, h, i])
            wait_all(fsend[p][h].at[pl.ds(TD, (C - 1) * TD)], f_s.at[p, h])
    for h in range(NC):
        wait_all(psend[h].at[pl.ds(TD, (C - 1) * TD)], p_s.at[h])
        gather_sent(group_at(h), g_s.at[h], h_s.at[h])
    for t in range(TD):
        pltpu.make_async_copy(tile_f32.at[t], tiles_out.at[t], local.at[1 + t]).wait()


def index_table(tile_rows, tile_cols, row, me):
    y, z = row // Z, row % Z
    tiles = C * TD
    of_group = lambda ids, g: lax.dynamic_slice(ids, (g * tiles,), (tiles,))
    cols = jnp.stack([of_group(tile_cols, ((y + d) % Y) * Z + z) for d in range(Y)])
    rows = of_group(tile_rows, row)
    source, local = cols // BLK, cols % BLK
    place = jnp.arange(tiles)
    rank = jnp.sum(
        (source[:, :, None] == source[:, None, :]) & (place[None, :] < place[:, None])[None],
        axis=2,
        dtype=jnp.int32,
    )
    slot = jnp.arange(SLOTS)
    chosen = (source[1:, None, :] == y * Z + slot[None, :, None] // CAP) & (
        rank[1:, None, :] == slot[None, :, None] % CAP
    )
    pick = jnp.sum(jnp.where(chosen, local[1:, None, :], 0), axis=2).reshape(-1)
    plane, depth = source[0] // Z, source[0] % Z
    away = (y - plane + Y) % Y
    fwd = jnp.where(
        away == 0,
        depth * BLK + local[0],
        PLANE + (away - 1) * SLOTS + depth * CAP + rank[0],
    )
    local_rows = rows - row * BLK
    before = (local_rows[None, :] < local_rows[:, None]) | (
        (local_rows[None, :] == local_rows[:, None]) & (place[None, :] < place[:, None])
    )
    position = jnp.sum(before, axis=1, dtype=jnp.int32)
    at = position[None, :] == place[:, None]
    lands = ((place // TD - me + C) % C) * TD + place % TD
    order = jnp.sum(jnp.where(at, lands[None, :], 0), axis=1)
    first = jnp.sum(local_rows[None, :] < local_rows[:, None], axis=1, dtype=jnp.int32)
    same = jnp.sum(jnp.where(at, (position > first)[None, :].astype(jnp.int32), 0), axis=1)
    blocks = jnp.arange(BLK)
    upto = jnp.sum(local_rows[None, :] <= blocks[:, None], axis=1, dtype=jnp.int32)
    count = jnp.sum(local_rows[None, :] == blocks[:, None], axis=1, dtype=jnp.int32)
    mine = (me * TD + jnp.arange(TD))[:, None] == place[None, :]
    my_rows = jnp.sum(jnp.where(mine, local_rows[None, :], 0), axis=1)
    on_diag = jnp.sum(jnp.where(mine, (rows == cols[0])[None, :].astype(jnp.int32), 0), axis=1)
    table = jnp.concatenate(
        [pick, fwd, order, same, jnp.maximum(upto - 1, 0), (count > 0).astype(jnp.int32), on_diag, my_rows]
    )
    return table.astype(jnp.int32)


def per_device(samples, loadings, omega_tiles, omega_diagonal, tile_rows, tile_cols):
    row = lax.axis_index("rows")
    me = lax.axis_index("cols")
    factors = loadings.shape[0]
    ns = NC * SC
    table = index_table(tile_rows, tile_cols, row, me)
    f32 = jnp.float32
    vmem = lambda *shape: pltpu.VMEM(shape, f32)
    dma = lambda *shape: pltpu.SemaphoreType.DMA(shape)
    in_vmem = pl.BlockSpec(memory_space=pltpu.VMEM)
    anywhere = pl.BlockSpec(memory_space=pl.ANY)
    n = 2 * NC
    new_tiles, new_diagonal = pl.pallas_call(
        route_kernel,
        out_shape=(
            jax.ShapeDtypeStruct(omega_tiles.shape, f32),
            jax.ShapeDtypeStruct((1, BLK * BS), f32),
        ),
        in_specs=[
            pl.BlockSpec(memory_space=pltpu.SMEM),
            in_vmem,
            in_vmem,
            in_vmem,
            anywhere,
        ],
        out_specs=(anywhere, in_vmem),
        scratch_shapes=[
            vmem(3, ns, factors),
            vmem(Z, ns, factors),
            vmem(Y, ns, factors),
            vmem(C, ns, factors),
            vmem(C, ns, BLK * BS),
            vmem(BLK, SC, BS),
            vmem(C * TD, SC, BS),
            vmem(TD, BS, BS),
            pltpu.VMEM((TD, BS, BS), jnp.bfloat16),
            pltpu.VMEM((TD, BS, BS), jnp.bfloat16),
        ]
        + [vmem(PLANE + (Y - 1) * SLOTS, SC, BS)] * n
        + [vmem((Y - 1) * SLOTS, SC, BS)] * n
        + [vmem(C * TD, SC, BS)] * n
        + [vmem(TD, C, SC, BS)] * n
        + [vmem(C, BLK, SC, BS)] * n
        + [vmem(C * TD, SC, BS)] * NC
        + [vmem(C * TD, SC, BS)] * NC
        + [
            dma(3),
            dma(3),
            dma(2, NC, 2),
            dma(2, NC, 2, Z // 2 + 1, 2),
            dma(2, NC, Y - 1),
            dma(2, NC, Y - 1),
            dma(2, NC),
            dma(2, NC, TD),
            dma(NC),
            dma(NC),
            dma(NC, C // 2),
            dma(NC, C // 2),
            dma(NC, C // 2),
            dma(NC, C // 2),
            dma(C // 2),
            dma(C // 2),
            dma(C // 2),
            dma(C // 2),
            dma(1 + TD),
        ],
        compiler_params=pltpu.CompilerParams(
            collective_id=0, has_side_effects=True, vmem_limit_bytes=46 * 1024 * 1024
        ),
        name="route",
    )(table, samples, loadings, omega_diagonal.reshape(1, BLK * BS), omega_tiles)

    limit = step_size * penalty
    new_tiles = new_tiles - jnp.clip(new_tiles, -limit, limit)
    return new_tiles, new_diagonal.reshape(-1)


def solution(mesh):
    placed = (
        P("cols", "rows"),
        P(None, "rows"),
        P(("rows", "cols"), None, None),
        P("rows"),
        P(),
        P(),
    )
    return jax.shard_map(
        per_device,
        mesh=mesh,
        in_specs=placed,
        out_specs=(P(("rows", "cols"), None, None), P("rows")),
        check_vma=False,
    )
```

```python
import functools
import jax
import jax.numpy as jnp
from jax import lax
from jax.experimental import pallas as pl
from jax.experimental.pallas import tpu as pltpu
from jax.sharding import PartitionSpec as P

step_size = 0.5
penalty = 0.02
MESH = pl.DeviceIdType.MESH
CAP = 3
Y = 4
Z = 8
C = 8
BLK = 8
TD = 5
NC = 2
SC = 8
BS = 512
PLANE = Z * BLK
SLOTS = Z * CAP

PICK = 0
FWD = PICK + (Y - 1) * SLOTS
ORDER = FWD + C * TD
SAME = ORDER + C * TD
LAST = SAME + C * TD
HAS = LAST + BLK
DIAG = HAS + BLK
ROWS = DIAG + TD
META = ROWS + TD


def split2(x):
    hi = x.astype(jnp.bfloat16)
    return hi, (x - hi.astype(jnp.float32)).astype(jnp.bfloat16)


def split3(x):
    hi, rest = x.astype(jnp.bfloat16), None
    rest = x - hi.astype(jnp.float32)
    mid, low = split2(rest)
    return jnp.concatenate([hi, mid, low], axis=0)


def dot(a, b, dims):
    return lax.dot_general(a, b, (dims, ((), ())), preferred_element_type=jnp.float32)


def wait_all(ref, sem):
    pltpu.make_async_copy(ref, ref, sem).wait()


def route_kernel(
    meta,
    samples_in,
    loadings_in,
    diag_in,
    tiles,
    tiles_out,
    diag_out,
    part,
    score_z,
    score_y,
    score_c,
    window,
    stage,
    seg,
    samples,
    loadings,
    diag,
    tile_f32,
    tile_hi,
    tile_lo,
    *rest,
):
    n = 2 * NC
    pair = lambda flat: (flat[:NC], flat[NC:])
    field, ysend, fsend, frecv, group = (pair(rest[i * n : (i + 1) * n]) for i in range(5))
    rest = rest[5 * n :]
    slots = (((rest[0], rest[1]), (rest[2],)), ((rest[3],), (rest[4], rest[5])))
    rest = rest[6:]
    psend, precv = rest[:NC], rest[NC : 2 * NC]
    (
        exch_s,
        exch_r,
        ring_s,
        ring_r,
        y_s,
        y_r,
        f_s,
        f_r,
        p_s,
        p_r,
        g_s,
        g_r,
        h_s,
        h_r,
        w_s,
        w_r,
        v_s,
        v_r,
        local,
    ) = rest[2 * NC :]

    row = lax.axis_index("rows")
    me = lax.axis_index("cols")
    y, z = row // Z, row % Z
    at_z = lambda d: {"rows": y * Z + (z + d + Z) % Z}
    at_y = lambda d: {"rows": ((y + d) % Y) * Z + z}
    at_c = lambda d: {"cols": (me + d + C) % C}
    side = 1 - 2 * (me % 2)
    other = at_c(side)

    def remote(src, dst, send, recv, where):
        return pltpu.make_async_remote_copy(
            src_ref=src,
            dst_ref=dst,
            send_sem=send,
            recv_sem=recv,
            device_id=where,
            device_id_type=MESH,
        )

    def each(low, high, body):
        lax.fori_loop(low, high, lambda i, _: (body(i), None)[1], None)

    barrier = pltpu.get_barrier_semaphore()

    def greet(where, count):
        each(
            1,
            count,
            lambda d: pl.semaphore_signal(
                barrier, inc=1, device_id=where(d), device_id_type=MESH
            ),
        )

    greet(at_z, Z)
    greet(at_y, Y)
    greet(at_c, C)
    loads = [
        pltpu.make_async_copy(src, dst, local.at[1 + TD + i])
        for i, (src, dst) in enumerate(
            ((samples_in, samples), (loadings_in, loadings), (diag_in, diag))
        )
    ]
    for load in loads:
        load.start()
    tile_copy = pltpu.make_async_copy(tiles, tile_f32, local.at[0])
    tile_copy.start()

    def split_tiles(low, high):
        rows = lax.broadcasted_iota(jnp.int32, (BS // 4, BS), 0)
        cols = lax.broadcasted_iota(jnp.int32, (BS // 4, BS), 1)

        def one(i):
            t, q = i // 4, i % 4
            at = pl.ds(pl.multiple_of(q * (BS // 4), BS // 4), BS // 4)
            flag = jnp.full((BS // 4, BS), meta[DIAG + t], jnp.int32)
            drop = (rows + q * (BS // 4) == cols) & (flag != 0)
            hi, lo = split2(jnp.where(drop, 0.0, tile_f32[t, at]))
            tile_hi[t, at] = hi
            tile_lo[t, at] = lo

        each(low, high, one)

    def score_step(b, total):
        cols = pl.ds(pl.multiple_of(b * BS, BS), BS)
        return total + dot(split3(samples[:, cols]), loadings[:, cols], ((1,), (1,)))

    for load in loads:
        load.wait()
    ns = NC * SC
    total = lax.fori_loop(0, BLK, score_step, jnp.zeros((3 * ns, loadings.shape[0]), jnp.float32))
    part[0] = total[:ns] + total[ns : 2 * ns] + total[2 * ns :]
    pl.semaphore_wait(barrier, Z + Y + C - 3)

    def gather_start(src, place, far_s, far_r, near_s, near_r):
        each(
            1,
            C // 2,
            lambda q: remote(src, place(2 * q), far_s.at[q], far_r.at[q], at_c(2 * q)).start(),
        )
        remote(src, place((side + C) % C), near_s.at[0], near_r.at[0], other).start()

    def gather_pass(place, far_r, near_s, near_r):
        def one(q):
            wait_all(place(2 * q), far_r.at[q])
            remote(
                place(2 * q), place((side + 2 * q + C) % C), near_s.at[q], near_r.at[q], other
            ).start()

        each(1, C // 2, one)

    def gathered(place, near_r):
        each(0, C // 2, lambda q: wait_all(place((2 * q - side + C) % C), near_r.at[q]))

    def gather_sent(place, far_s, near_s):
        each(1, C // 2, lambda q: wait_all(place(2 * q), far_s.at[q]))
        each(0, C // 2, lambda q: wait_all(place(2 * q), near_s.at[q]))

    window_at = lambda d: window.at[d]

    each(
        1,
        Z,
        lambda d: remote(part.at[0], score_z.at[d], exch_s.at[0], exch_r.at[0], at_z(d)).start(),
    )
    gather_start(samples, window_at, w_s, w_r, v_s, v_r)
    tile_copy.wait()
    split_tiles(0, 12)
    wait_all(score_z.at[pl.ds(1, Z - 1)], exch_r.at[0])
    total = part[0]
    for d in range(1, Z):
        total = total + score_z[d]
    part[1] = total
    each(
        1,
        Y,
        lambda d: remote(part.at[1], score_y.at[d], exch_s.at[1], exch_r.at[1], at_y(d)).start(),
    )
    split_tiles(12, TD * 4)
    wait_all(score_y.at[pl.ds(1, Y - 1)], exch_r.at[1])
    for d in range(1, Y):
        total = total + score_y[d]
    scores = split3(total)
    part[2] = total

    def residual_step(b):
        cols = pl.ds(pl.multiple_of(b * BS, BS), BS)
        terms = dot(scores, loadings[:, cols], ((1,), (0,)))
        value = samples[:, cols] - (terms[:ns] + terms[ns : 2 * ns] + terms[2 * ns :])
        for h in range(NC):
            field[0][h][z * BLK + b] = value[h * SC : (h + 1) * SC]
            group[0][h][0, b] = value[h * SC : (h + 1) * SC]

    each(0, BLK, residual_step)

    def group_residual():
        gathered(window_at, v_r)
        wait_all(score_c.at[pl.ds(1, C - 1)], exch_r.at[2])
        far = (C - 1) * ns
        terms3 = split3(score_c[1:].reshape(far, loadings.shape[0]))

        def one(b):
            cols = pl.ds(pl.multiple_of(b * BS, BS), BS)
            terms = dot(terms3, loadings[:, cols], ((1,), (0,)))
            terms = terms[:far] + terms[far : 2 * far] + terms[2 * far :]
            value = window[pl.ds(1, C - 1), :, cols] - terms.reshape(C - 1, ns, BS)
            for h in range(NC):
                group[0][h][pl.ds(1, C - 1), b] = value[:, h * SC : (h + 1) * SC]

        each(0, BLK, one)

    half = BLK // 2

    def hop(p, h, k, u, right):
        slice_of = ((z - k + 1 + Z) if right else (z + k - 1)) % Z
        ref = field[p][h].at[pl.ds(slice_of * BLK + u * half, half)]
        way = 0 if right else 1
        return remote(
            ref,
            ref,
            ring_s.at[p, h, way],
            ring_r.at[p, h, way, k, u],
            at_z(1 if right else -1),
        )

    def arrived(p, h, k, u, right):
        slice_of = ((z - k + Z) if right else (z + k)) % Z
        ref = field[p][h].at[pl.ds(slice_of * BLK + u * half, half)]
        wait_all(ref, ring_r.at[p, h, 0 if right else 1, k, u])

    def part_of(q):
        return pl.ds(0, BS) if q is None else pl.ds(q * (BS // 2), BS // 2)

    def send_slots(p, h, zs, i, q):
        base = i * SLOTS + zs * CAP
        remote(
            ysend[p][h].at[pl.ds(base, CAP), :, part_of(q)],
            slots[p][h][q or 0].at[pl.ds(base, CAP)],
            y_s.at[p, h, i],
            y_r.at[p, h, i, q or 0],
            at_y(i + 1),
        ).start()

    def send_picks(p, h, zs, q=None):
        stage[...] = field[p][h][pl.ds(zs * BLK, BLK)]

        def to_plane(i):
            base = i * SLOTS + zs * CAP
            for j in range(CAP):
                ysend[p][h][base + j] = stage[meta[PICK + base + j]]
            send_slots(p, h, zs, i, q)

        each(0, Y - 1, to_plane)

    def send_rest(p, h):
        each(0, Z * (Y - 1), lambda a: send_slots(p, h, (z + a // (Y - 1)) % Z, a % (Y - 1), 1))

    def ring_start(p, h):
        for u in range(2):
            hop(p, h, 1, u, True).start()
            hop(p, h, 1, 1 - u, False).start()

    def ring_step(p, h, k, last=False, q=None):
        for u in range(2):
            arrived(p, h, k, u, True)
            if not last or u == 0:
                hop(p, h, k + 1, u, True).start()
            arrived(p, h, k, 1 - u, False)
            if not last or u == 0:
                hop(p, h, k + 1, 1 - u, False).start()
        picks_at(p, h, k, q)

    def ring_end(p, h, q=None):
        arrived(p, h, Z // 2, 0, True)
        arrived(p, h, Z // 2, 1, False)
        send_picks(p, h, (z + Z // 2) % Z, q)

    def picks_at(p, h, k, q):
        send_picks(p, h, (z - k + Z) % Z, q)
        send_picks(p, h, (z + k) % Z, q)

    def routed(p, h, q=None):
        for i in range(Y - 1):
            wait_all(slots[p][h][q or 0].at[pl.ds(i * SLOTS, SLOTS)], y_r.at[p, h, i, q or 0])

    def block_of(p, h, at, q):
        own = jnp.full((SC, BS if q is None else BS // 2), at, jnp.int32) < PLANE
        near = field[p][h][jnp.minimum(at, PLANE - 1), :, part_of(q)]
        return jnp.where(own, near, slots[p][h][q or 0][jnp.maximum(at - PLANE, 0)])

    def forward(p, h, q=None):
        cols = part_of(q)

        def tile(t):
            def one(d):
                dest = (me + d) % C
                at = d * TD + t
                fsend[p][h][at, :, cols] = block_of(p, h, meta[FWD + dest * TD + t], q)
                remote(
                    fsend[p][h].at[at, :, cols],
                    frecv[p][h].at[t, d, :, cols],
                    f_s.at[p, h],
                    f_r.at[p, h, t],
                    at_c(d),
                ).start()

            each(1, C, one)
            frecv[p][h][t, 0, :, cols] = block_of(p, h, meta[FWD + me * TD + t], q)

        each(0, TD, tile)

    def forward_half(p, h):
        cols = part_of(0)

        def one(d):
            dest = (me + d) % C
            for t in range(TD):
                at = d * TD + t
                fsend[p][h][at, :, cols] = block_of(p, h, meta[FWD + dest * TD + t], 0)
            remote(
                fsend[p][h].at[pl.ds(d * TD, TD), :, cols],
                frecv[p][h].at[:, d, :, cols],
                f_s.at[p, h],
                f_r.at[p, h, TD],
                at_c(d),
            ).start()

        each(1, C, one)
        for t in range(TD):
            frecv[p][h][t, 0, :, cols] = block_of(p, h, meta[FWD + me * TD + t], 0)

    def forwarded(p, h, t, q=None):
        wait_all(frecv[p][h].at[t, pl.ds(1, C - 1), :, part_of(q)], f_r.at[p, h, t])

    def forwarded_half(p, h):
        wait_all(frecv[p][h].at[:, pl.ds(1, C - 1), :, part_of(0)], f_r.at[p, h, TD])

    def products(h):
        if h == 0:
            forwarded_half(0, h)

        def one(t):
            forwarded(0, h, t, 1 if h == 0 else None)
            hi, lo = split2(frecv[0][h][t].reshape(C * SC, BS))
            both = dot(jnp.concatenate([hi, lo], axis=0), tile_hi[t], ((1,), (1,)))
            value = both[: C * SC] + both[C * SC :] + dot(hi, tile_lo[t], ((1,), (1,)))
            value = value.reshape(C, SC, BS)
            precv[h][t] = value[0]
            for d in range(1, C):
                psend[h][d * TD + t] = value[d]
            each(
                1,
                C,
                lambda d: remote(
                    psend[h].at[d * TD + t],
                    precv[h].at[d * TD + t],
                    p_s.at[h],
                    p_r.at[h],
                    at_c(-d),
                ).start(),
            )

        each(0, TD, one)

    def apply_rows(h):
        wait_all(precv[h].at[pl.ds(TD, (C - 1) * TD)], p_r.at[h])

        def one(k, running):
            same = jnp.full((SC, BS), meta[SAME + k], jnp.int32) != 0
            running = jnp.where(same, running, 0.0) + precv[h][meta[ORDER + k]]
            seg[k] = running
            return running

        lax.fori_loop(0, C * TD, one, jnp.zeros((SC, BS), jnp.float32))

        def block(b):
            has = jnp.full((SC, BS), meta[HAS + b], jnp.int32) != 0
            value = jnp.where(has, seg[meta[LAST + b]], 0.0)
            value = value + diag[:, pl.ds(pl.multiple_of(b * BS, BS), BS)] * group[0][h][0, b]
            field[1][h][z * BLK + b] = value
            group[1][h][0, b] = value

        each(0, BLK, block)

    group_at = lambda h: lambda d: group[1][h].at[d]

    def rows_start(h):
        gather_start(group[1][h].at[0], group_at(h), g_s.at[h], g_r.at[h], h_s.at[h], h_r.at[h])

    def rows_pass(h):
        gather_pass(group_at(h), g_r.at[h], h_s.at[h], h_r.at[h])

    scale = step_size * 0.5 / (NC * C * SC)

    def gradient_step(h, q=None):
        cols = part_of(q)
        width = BS if q is None else BS // 2
        if q == 0:
            forwarded_half(1, h)

        def one(t):
            if q != 0:
                forwarded(1, h, t, q)
            block = meta[ROWS + t]
            rows = lambda p: group[p][h][:, block].reshape(C * SC, BS)
            left_hi, left_lo = split2(jnp.concatenate([rows(1), rows(0)], axis=0))
            right = [frecv[p][h][t, :, :, cols].reshape(C * SC, width) for p in range(2)]
            right_hi, right_lo = split2(jnp.concatenate(right, axis=0))
            left = jnp.concatenate([left_hi, left_hi, left_lo], axis=0)
            right = jnp.concatenate([right_hi, right_lo, right_hi], axis=0)
            total = dot(left, right, ((0,), (0,)))
            stepped = tile_f32[t, :, cols] - scale * total
            if q is not None:
                i = lax.broadcasted_iota(jnp.int32, (BS, width), 0)
                j = lax.broadcasted_iota(jnp.int32, (BS, width), 1) + q * width
                flag = jnp.full((BS, width), meta[DIAG + t], jnp.int32)
                stepped = jnp.where((i == j) & (flag != 0), 0.0, stepped)
            tile_f32[t, :, cols] = stepped
            if q == 1:
                pltpu.make_async_copy(tile_f32.at[t], tiles_out.at[t], local.at[1 + t]).start()

        each(0, TD, one)

    def diag_step(b):
        total = jnp.zeros((SC, BS), jnp.float32)
        for h in range(NC):
            for d in range(C):
                total = total + group[0][h][d, b] * group[1][h][d, b]
        stat = jnp.sum(total, axis=0, keepdims=True) / (NC * C * SC)
        at = pl.ds(pl.multiple_of(b * BS, BS), BS)
        old = diag[:, at]
        diag_out[:, at] = old - step_size * (stat - 1.0 / old)

    far_step = Z // 2 - 1

    ring_start(0, 0)
    send_picks(0, 0, z, 0)
    send_picks(0, 1, z)
    each(
        1,
        C,
        lambda d: remote(part.at[2], score_c.at[d], exch_s.at[2], exch_r.at[2], at_c(d)).start(),
    )
    each(1, far_step, lambda k: ring_step(0, 0, k, q=0))
    ring_step(0, 0, far_step, last=True, q=0)
    ring_start(0, 1)
    gather_pass(window_at, w_r, v_s, v_r)
    ring_end(0, 0, 0)
    send_rest(0, 0)
    routed(0, 0, 0)
    forward_half(0, 0)
    each(1, far_step, lambda k: ring_step(0, 1, k))
    ring_step(0, 1, far_step, last=True)
    ring_end(0, 1)
    routed(0, 0, 1)
    forward(0, 0, 1)
    products(0)
    group_residual()

    apply_rows(0)
    ring_start(1, 0)
    send_picks(1, 0, z)
    routed(0, 1)
    forward(0, 1)
    rows_start(0)
    each(1, far_step, lambda k: ring_step(1, 0, k))
    ring_step(1, 0, far_step, last=True)
    products(1)
    ring_end(1, 0)
    rows_pass(0)

    apply_rows(1)
    ring_start(1, 1)
    send_picks(1, 1, z, 0)
    routed(1, 0)
    forward(1, 0)
    rows_start(1)
    each(1, far_step, lambda k: ring_step(1, 1, k, q=0))
    ring_step(1, 1, far_step, last=True, q=0)
    ring_end(1, 1, 0)
    send_rest(1, 1)
    rows_pass(1)
    gathered(group_at(0), h_r.at[0])
    gradient_step(0)
    gathered(group_at(1), h_r.at[1])
    each(0, BLK, diag_step)
    routed(1, 1, 0)
    forward_half(1, 1)
    gradient_step(1, 0)
    routed(1, 1, 1)
    forward(1, 1, 1)
    gradient_step(1, 1)

    wait_all(score_z.at[pl.ds(1, Z - 1)], exch_s.at[0])
    wait_all(score_y.at[pl.ds(1, Y - 1)], exch_s.at[1])
    wait_all(score_c.at[pl.ds(1, C - 1)], exch_s.at[2])
    gather_sent(window_at, w_s, v_s)
    sent = Z // 2 * BLK - BLK // 2
    for p in range(2):
        for h in range(NC):
            for way in range(2):
                wait_all(field[p][h].at[pl.ds(0, sent)], ring_s.at[p, h, way])
            for i in range(Y - 1):
                wait_all(ysend[p][h].at[pl.ds(i * SLOTS, SLOTS)], y_s.at[p, h, i])
            wait_all(fsend[p][h].at[pl.ds(TD, (C - 1) * TD)], f_s.at[p, h])
    for h in range(NC):
        wait_all(psend[h].at[pl.ds(TD, (C - 1) * TD)], p_s.at[h])
        gather_sent(group_at(h), g_s.at[h], h_s.at[h])
    for t in range(TD):
        pltpu.make_async_copy(tile_f32.at[t], tiles_out.at[t], local.at[1 + t]).wait()


def index_table(tile_rows, tile_cols, row, me):
    y, z = row // Z, row % Z
    tiles = C * TD
    of_group = lambda ids, g: lax.dynamic_slice(ids, (g * tiles,), (tiles,))
    slices = [of_group(tile_cols, ((y + d) % Y) * Z + z) for d in range(Y)]
    *slices, rows = lax.optimization_barrier((*slices, of_group(tile_rows, row)))
    cols = jnp.stack(slices)
    source, local = cols // BLK, cols % BLK
    place = jnp.arange(tiles)
    rank = jnp.sum(
        (source[:, :, None] == source[:, None, :]) & (place[None, :] < place[:, None])[None],
        axis=2,
        dtype=jnp.int32,
    )
    slot = jnp.arange(SLOTS)
    chosen = (source[1:, None, :] == y * Z + slot[None, :, None] // CAP) & (
        rank[1:, None, :] == slot[None, :, None] % CAP
    )
    pick = jnp.sum(jnp.where(chosen, local[1:, None, :], 0), axis=2).reshape(-1)
    plane, depth = source[0] // Z, source[0] % Z
    away = (y - plane + Y) % Y
    fwd = jnp.where(
        away == 0,
        depth * BLK + local[0],
        PLANE + (away - 1) * SLOTS + depth * CAP + rank[0],
    )
    local_rows = rows - row * BLK
    before = (local_rows[None, :] < local_rows[:, None]) | (
        (local_rows[None, :] == local_rows[:, None]) & (place[None, :] < place[:, None])
    )
    position = jnp.sum(before, axis=1, dtype=jnp.int32)
    at = position[None, :] == place[:, None]
    lands = ((place // TD - me + C) % C) * TD + place % TD
    order = jnp.sum(jnp.where(at, lands[None, :], 0), axis=1)
    first = jnp.sum(local_rows[None, :] < local_rows[:, None], axis=1, dtype=jnp.int32)
    same = jnp.sum(jnp.where(at, (position > first)[None, :].astype(jnp.int32), 0), axis=1)
    blocks = jnp.arange(BLK)
    upto = jnp.sum(local_rows[None, :] <= blocks[:, None], axis=1, dtype=jnp.int32)
    count = jnp.sum(local_rows[None, :] == blocks[:, None], axis=1, dtype=jnp.int32)
    mine = (me * TD + jnp.arange(TD))[:, None] == place[None, :]
    my_rows = jnp.sum(jnp.where(mine, local_rows[None, :], 0), axis=1)
    on_diag = jnp.sum(jnp.where(mine, (rows == cols[0])[None, :].astype(jnp.int32), 0), axis=1)
    table = jnp.concatenate(
        [pick, fwd, order, same, jnp.maximum(upto - 1, 0), (count > 0).astype(jnp.int32), on_diag, my_rows]
    )
    return table.astype(jnp.int32)


def per_device(samples, loadings, omega_tiles, omega_diagonal, tile_rows, tile_cols):
    row = lax.axis_index("rows")
    me = lax.axis_index("cols")
    factors = loadings.shape[0]
    ns = NC * SC
    table = index_table(tile_rows, tile_cols, row, me)
    f32 = jnp.float32
    vmem = lambda *shape: pltpu.VMEM(shape, f32)
    dma = lambda *shape: pltpu.SemaphoreType.DMA(shape)
    in_vmem = pl.BlockSpec(memory_space=pltpu.VMEM)
    in_hbm = pl.BlockSpec(memory_space=pltpu.HBM)
    anywhere = pl.BlockSpec(memory_space=pl.ANY)
    n = 2 * NC
    new_tiles, new_diagonal = pl.pallas_call(
        route_kernel,
        out_shape=(
            jax.ShapeDtypeStruct(omega_tiles.shape, f32),
            jax.ShapeDtypeStruct((1, BLK * BS), f32),
        ),
        in_specs=[
            pl.BlockSpec(memory_space=pltpu.SMEM),
            in_hbm,
            in_hbm,
            in_hbm,
            in_hbm,
        ],
        out_specs=(anywhere, in_vmem),
        scratch_shapes=[
            vmem(3, ns, factors),
            vmem(Z, ns, factors),
            vmem(Y, ns, factors),
            vmem(C, ns, factors),
            vmem(C, ns, BLK * BS),
            vmem(BLK, SC, BS),
            vmem(C * TD, SC, BS),
            vmem(ns, BLK * BS),
            pltpu.VMEM(loadings.shape, jnp.bfloat16),
            vmem(1, BLK * BS),
            vmem(TD, BS, BS),
            pltpu.VMEM((TD, BS, BS), jnp.bfloat16),
            pltpu.VMEM((TD, BS, BS), jnp.bfloat16),
        ]
        + [vmem(PLANE, SC, BS)] * n
        + [vmem((Y - 1) * SLOTS, SC, BS)] * n
        + [vmem(C * TD, SC, BS)] * n
        + [vmem(TD, C, SC, BS)] * n
        + [vmem(C, BLK, SC, BS)] * n
        + [vmem((Y - 1) * SLOTS, SC, BS // parts) for parts in (2, 2, 1, 1, 2, 2)]
        + [vmem(C * TD, SC, BS)] * NC
        + [vmem(C * TD, SC, BS)] * NC
        + [
            dma(3),
            dma(3),
            dma(2, NC, 2),
            dma(2, NC, 2, Z // 2 + 1, 2),
            dma(2, NC, Y - 1),
            dma(2, NC, Y - 1, 2),
            dma(2, NC),
            dma(2, NC, TD + 1),
            dma(NC),
            dma(NC),
            dma(NC, C // 2),
            dma(NC, C // 2),
            dma(NC, C // 2),
            dma(NC, C // 2),
            dma(C // 2),
            dma(C // 2),
            dma(C // 2),
            dma(C // 2),
            dma(4 + TD),
        ],
        compiler_params=pltpu.CompilerParams(
            collective_id=0, has_side_effects=True, vmem_limit_bytes=46 * 1024 * 1024
        ),
        name="route",
    )(
        table,
        *(
            pltpu.with_memory_space_constraint(x, pltpu.HBM)
            for x in (samples, loadings, omega_diagonal.reshape(1, BLK * BS), omega_tiles)
        ),
    )

    limit = step_size * penalty
    new_tiles = new_tiles - jnp.clip(new_tiles, -limit, limit)
    return new_tiles, new_diagonal.reshape(-1)


def solution(mesh):
    placed = (
        P("cols", "rows"),
        P(None, "rows"),
        P(("rows", "cols"), None, None),
        P("rows"),
        P(),
        P(),
    )
    return jax.shard_map(
        per_device,
        mesh=mesh,
        in_specs=placed,
        out_specs=(P(("rows", "cols"), None, None), P("rows")),
        check_vma=False,
    )
```

```python
import functools
import jax
import jax.numpy as jnp
from jax import lax
from jax.experimental import pallas as pl
from jax.experimental.pallas import tpu as pltpu
from jax.sharding import PartitionSpec as P

step_size = 0.5
penalty = 0.02
MESH = pl.DeviceIdType.MESH
CAP = 3
Y = 4
Z = 8
C = 8
BLK = 8
TD = 5
NC = 2
SC = 8
BS = 512
PLANE = Z * BLK
SLOTS = Z * CAP

PICK = 0
FWD = PICK + (Y - 1) * SLOTS
ORDER = FWD + C * TD
SAME = ORDER + C * TD
LAST = SAME + C * TD
HAS = LAST + BLK
DIAG = HAS + BLK
ROWS = DIAG + TD
META = ROWS + TD


def split2(x):
    hi = x.astype(jnp.bfloat16)
    return hi, (x - hi.astype(jnp.float32)).astype(jnp.bfloat16)


def split3(x):
    hi, rest = x.astype(jnp.bfloat16), None
    rest = x - hi.astype(jnp.float32)
    mid, low = split2(rest)
    return jnp.concatenate([hi, mid, low], axis=0)


def dot(a, b, dims):
    return lax.dot_general(a, b, (dims, ((), ())), preferred_element_type=jnp.float32)


def wait_all(ref, sem):
    pltpu.make_async_copy(ref, ref, sem).wait()


def route_kernel(
    meta,
    samples_in,
    loadings_in,
    diag_in,
    tiles,
    tiles_out,
    diag_out,
    part,
    score_z,
    score_y,
    score_c,
    window,
    stage,
    seg,
    samples,
    loadings,
    diag,
    tile_f32,
    tile_hi,
    tile_lo,
    *rest,
):
    n = 2 * NC
    pair = lambda flat: (flat[:NC], flat[NC:])
    field, ysend, fsend, frecv, group = (pair(rest[i * n : (i + 1) * n]) for i in range(5))
    rest = rest[5 * n :]
    psend, precv = rest[:NC], rest[NC : 2 * NC]
    (
        exch_s,
        exch_r,
        ring_s,
        ring_r,
        y_s,
        y_r,
        f_s,
        f_r,
        p_s,
        p_r,
        g_s,
        g_r,
        h_s,
        h_r,
        w_s,
        w_r,
        v_s,
        v_r,
        local,
    ) = rest[2 * NC :]

    row = lax.axis_index("rows")
    me = lax.axis_index("cols")
    y, z = row // Z, row % Z
    at_z = lambda d: {"rows": y * Z + (z + d + Z) % Z}
    at_y = lambda d: {"rows": ((y + d) % Y) * Z + z}
    at_c = lambda d: {"cols": (me + d + C) % C}
    side = 1 - 2 * (me % 2)
    other = at_c(side)

    def remote(src, dst, send, recv, where):
        return pltpu.make_async_remote_copy(
            src_ref=src,
            dst_ref=dst,
            send_sem=send,
            recv_sem=recv,
            device_id=where,
            device_id_type=MESH,
        )

    def each(low, high, body):
        lax.fori_loop(low, high, lambda i, _: (body(i), None)[1], None)

    barrier = pltpu.get_barrier_semaphore()

    def greet(where, count):
        each(
            1,
            count,
            lambda d: pl.semaphore_signal(
                barrier, inc=1, device_id=where(d), device_id_type=MESH
            ),
        )

    greet(at_z, Z)
    greet(at_y, Y)
    greet(at_c, C)
    loads = [
        pltpu.make_async_copy(src, dst, local.at[1 + TD + i])
        for i, (src, dst) in enumerate(
            ((samples_in, samples), (loadings_in, loadings), (diag_in, diag))
        )
    ]
    for load in loads:
        load.start()
    tile_copy = pltpu.make_async_copy(tiles, tile_f32, local.at[0])
    tile_copy.start()

    def split_tiles(low, high):
        rows = lax.broadcasted_iota(jnp.int32, (BS // 4, BS), 0)
        cols = lax.broadcasted_iota(jnp.int32, (BS // 4, BS), 1)

        def one(i):
            t, q = i // 4, i % 4
            at = pl.ds(pl.multiple_of(q * (BS // 4), BS // 4), BS // 4)
            flag = jnp.full((BS // 4, BS), meta[DIAG + t], jnp.int32)
            drop = (rows + q * (BS // 4) == cols) & (flag != 0)
            hi, lo = split2(jnp.where(drop, 0.0, tile_f32[t, at]))
            tile_hi[t, at] = hi
            tile_lo[t, at] = lo

        each(low, high, one)

    def score_step(b, total):
        cols = pl.ds(pl.multiple_of(b * BS, BS), BS)
        return total + dot(split3(samples[:, cols]), loadings[:, cols], ((1,), (1,)))

    for load in loads:
        load.wait()
    ns = NC * SC
    total = lax.fori_loop(0, BLK, score_step, jnp.zeros((3 * ns, loadings.shape[0]), jnp.float32))
    part[0] = total[:ns] + total[ns : 2 * ns] + total[2 * ns :]
    pl.semaphore_wait(barrier, Z + Y + C - 3)

    def gather_start(src, place, far_s, far_r, near_s, near_r):
        each(
            1,
            C // 2,
            lambda q: remote(src, place(2 * q), far_s.at[q], far_r.at[q], at_c(2 * q)).start(),
        )
        remote(src, place((side + C) % C), near_s.at[0], near_r.at[0], other).start()

    def gather_pass(place, far_r, near_s, near_r):
        def one(q):
            wait_all(place(2 * q), far_r.at[q])
            remote(
                place(2 * q), place((side + 2 * q + C) % C), near_s.at[q], near_r.at[q], other
            ).start()

        each(1, C // 2, one)

    def gathered(place, near_r):
        each(0, C // 2, lambda q: wait_all(place((2 * q - side + C) % C), near_r.at[q]))

    def gather_sent(place, far_s, near_s):
        each(1, C // 2, lambda q: wait_all(place(2 * q), far_s.at[q]))
        each(0, C // 2, lambda q: wait_all(place(2 * q), near_s.at[q]))

    window_at = lambda d: window.at[d]

    each(
        1,
        Z,
        lambda d: remote(part.at[0], score_z.at[d], exch_s.at[0], exch_r.at[0], at_z(d)).start(),
    )
    gather_start(samples, window_at, w_s, w_r, v_s, v_r)
    tile_copy.wait()
    split_tiles(0, 12)
    wait_all(score_z.at[pl.ds(1, Z - 1)], exch_r.at[0])
    total = part[0]
    for d in range(1, Z):
        total = total + score_z[d]
    part[1] = total
    each(
        1,
        Y,
        lambda d: remote(part.at[1], score_y.at[d], exch_s.at[1], exch_r.at[1], at_y(d)).start(),
    )
    split_tiles(12, TD * 4)
    wait_all(score_y.at[pl.ds(1, Y - 1)], exch_r.at[1])
    for d in range(1, Y):
        total = total + score_y[d]
    scores = split3(total)
    part[2] = total

    def residual_step(b):
        cols = pl.ds(pl.multiple_of(b * BS, BS), BS)
        terms = dot(scores, loadings[:, cols], ((1,), (0,)))
        value = samples[:, cols] - (terms[:ns] + terms[ns : 2 * ns] + terms[2 * ns :])
        for h in range(NC):
            field[0][h][z * BLK + b] = value[h * SC : (h + 1) * SC]
            group[0][h][0, b] = value[h * SC : (h + 1) * SC]

    each(0, BLK, residual_step)

    def group_residual():
        gathered(window_at, v_r)
        wait_all(score_c.at[pl.ds(1, C - 1)], exch_r.at[2])
        far = (C - 1) * ns
        terms3 = split3(score_c[1:].reshape(far, loadings.shape[0]))

        def one(b):
            cols = pl.ds(pl.multiple_of(b * BS, BS), BS)
            terms = dot(terms3, loadings[:, cols], ((1,), (0,)))
            terms = terms[:far] + terms[far : 2 * far] + terms[2 * far :]
            value = window[pl.ds(1, C - 1), :, cols] - terms.reshape(C - 1, ns, BS)
            for h in range(NC):
                group[0][h][pl.ds(1, C - 1), b] = value[:, h * SC : (h + 1) * SC]

        each(0, BLK, one)

    half = BLK // 2

    def hop(p, h, k, u, right):
        slice_of = ((z - k + 1 + Z) if right else (z + k - 1)) % Z
        ref = field[p][h].at[pl.ds(slice_of * BLK + u * half, half)]
        way = 0 if right else 1
        return remote(
            ref,
            ref,
            ring_s.at[p, h, way],
            ring_r.at[p, h, way, k, u],
            at_z(1 if right else -1),
        )

    def arrived(p, h, k, u, right):
        slice_of = ((z - k + Z) if right else (z + k)) % Z
        ref = field[p][h].at[pl.ds(slice_of * BLK + u * half, half)]
        wait_all(ref, ring_r.at[p, h, 0 if right else 1, k, u])

    def send_picks(p, h, zs):
        ref = field[p][h]
        stage[...] = ref[pl.ds(zs * BLK, BLK)]

        def to_plane(i):
            base = i * SLOTS + zs * CAP
            for j in range(CAP):
                ysend[p][h][base + j] = stage[meta[PICK + base + j]]
            remote(
                ysend[p][h].at[pl.ds(base, CAP)],
                ref.at[pl.ds(PLANE + base, CAP)],
                y_s.at[p, h, i],
                y_r.at[p, h, i],
                at_y(i + 1),
            ).start()

        each(0, Y - 1, to_plane)

    def ring_start(p, h):
        for u in range(2):
            hop(p, h, 1, u, True).start()
            hop(p, h, 1, 1 - u, False).start()

    def ring_step(p, h, k, last=False):
        for u in range(2):
            arrived(p, h, k, u, True)
            if not last or u == 0:
                hop(p, h, k + 1, u, True).start()
            arrived(p, h, k, 1 - u, False)
            if not last or u == 0:
                hop(p, h, k + 1, 1 - u, False).start()
        picks_at(p, h, k)

    def ring_end(p, h):
        arrived(p, h, Z // 2, 0, True)
        arrived(p, h, Z // 2, 1, False)
        send_picks(p, h, (z + Z // 2) % Z)

    def picks_at(p, h, k):
        send_picks(p, h, (z - k + Z) % Z)
        send_picks(p, h, (z + k) % Z)

    def routed(p, h):
        for i in range(Y - 1):
            wait_all(field[p][h].at[pl.ds(PLANE + i * SLOTS, SLOTS)], y_r.at[p, h, i])

    def forward(p, h):
        def tile(t):
            def one(d):
                dest = (me + d) % C
                at = d * TD + t
                fsend[p][h][at] = field[p][h][meta[FWD + dest * TD + t]]
                remote(
                    fsend[p][h].at[at],
                    frecv[p][h].at[t, d],
                    f_s.at[p, h],
                    f_r.at[p, h, t],
                    at_c(d),
                ).start()

            each(1, C, one)
            frecv[p][h][t, 0] = field[p][h][meta[FWD + me * TD + t]]

        each(0, TD, tile)

    def forwarded(p, h, t):
        wait_all(frecv[p][h].at[t, pl.ds(1, C - 1)], f_r.at[p, h, t])

    def products(h):
        def one(t):
            forwarded(0, h, t)
            hi, lo = split2(frecv[0][h][t].reshape(C * SC, BS))
            both = dot(jnp.concatenate([hi, lo], axis=0), tile_hi[t], ((1,), (1,)))
            value = both[: C * SC] + both[C * SC :] + dot(hi, tile_lo[t], ((1,), (1,)))
            value = value.reshape(C, SC, BS)
            precv[h][t] = value[0]
            for d in range(1, C):
                psend[h][d * TD + t] = value[d]
            each(
                1,
                C,
                lambda d: remote(
                    psend[h].at[d * TD + t],
                    precv[h].at[d * TD + t],
                    p_s.at[h],
                    p_r.at[h],
                    at_c(-d),
                ).start(),
            )

        each(0, TD, one)

    def apply_rows(h):
        wait_all(precv[h].at[pl.ds(TD, (C - 1) * TD)], p_r.at[h])

        def one(k, running):
            same = jnp.full((SC, BS), meta[SAME + k], jnp.int32) != 0
            running = jnp.where(same, running, 0.0) + precv[h][meta[ORDER + k]]
            seg[k] = running
            return running

        lax.fori_loop(0, C * TD, one, jnp.zeros((SC, BS), jnp.float32))

        def block(b):
            has = jnp.full((SC, BS), meta[HAS + b], jnp.int32) != 0
            value = jnp.where(has, seg[meta[LAST + b]], 0.0)
            value = value + diag[:, pl.ds(pl.multiple_of(b * BS, BS), BS)] * group[0][h][0, b]
            field[1][h][z * BLK + b] = value
            group[1][h][0, b] = value

        each(0, BLK, block)

    group_at = lambda h: lambda d: group[1][h].at[d]

    def rows_start(h):
        gather_start(group[1][h].at[0], group_at(h), g_s.at[h], g_r.at[h], h_s.at[h], h_r.at[h])

    def rows_pass(h):
        gather_pass(group_at(h), g_r.at[h], h_s.at[h], h_r.at[h])

    scale = step_size * 0.5 / (NC * C * SC)

    def gradient_step(h, finish):
        def one(t):
            forwarded(1, h, t)
            block = meta[ROWS + t]
            rows = lambda p: group[p][h][:, block].reshape(C * SC, BS)
            left_hi, left_lo = split2(jnp.concatenate([rows(1), rows(0)], axis=0))
            right = [frecv[p][h][t].reshape(C * SC, BS) for p in range(2)]
            right_hi, right_lo = split2(jnp.concatenate(right, axis=0))
            left = jnp.concatenate([left_hi, left_hi, left_lo], axis=0)
            right = jnp.concatenate([right_hi, right_lo, right_hi], axis=0)
            total = dot(left, right, ((0,), (0,)))
            stepped = tile_f32[t] - scale * total
            if finish:
                i = lax.broadcasted_iota(jnp.int32, (BS, BS), 0)
                j = lax.broadcasted_iota(jnp.int32, (BS, BS), 1)
                flag = jnp.full((BS, BS), meta[DIAG + t], jnp.int32)
                stepped = jnp.where((i == j) & (flag != 0), 0.0, stepped)
            tile_f32[t] = stepped
            if finish:
                pltpu.make_async_copy(tile_f32.at[t], tiles_out.at[t], local.at[1 + t]).start()

        each(0, TD, one)

    def diag_step(b):
        total = jnp.zeros((SC, BS), jnp.float32)
        for h in range(NC):
            for d in range(C):
                total = total + group[0][h][d, b] * group[1][h][d, b]
        stat = jnp.sum(total, axis=0, keepdims=True) / (NC * C * SC)
        at = pl.ds(pl.multiple_of(b * BS, BS), BS)
        old = diag[:, at]
        diag_out[:, at] = old - step_size * (stat - 1.0 / old)

    far_step = Z // 2 - 1

    ring_start(0, 0)
    send_picks(0, 0, z)
    send_picks(0, 1, z)
    each(
        1,
        C,
        lambda d: remote(part.at[2], score_c.at[d], exch_s.at[2], exch_r.at[2], at_c(d)).start(),
    )
    each(1, far_step, lambda k: ring_step(0, 0, k))
    ring_step(0, 0, far_step, last=True)
    ring_start(0, 1)
    gather_pass(window_at, w_r, v_s, v_r)
    ring_end(0, 0)
    each(1, far_step, lambda k: ring_step(0, 1, k))
    routed(0, 0)
    forward(0, 0)
    ring_step(0, 1, far_step, last=True)
    ring_end(0, 1)
    products(0)
    group_residual()

    apply_rows(0)
    ring_start(1, 0)
    send_picks(1, 0, z)
    routed(0, 1)
    forward(0, 1)
    rows_start(0)
    each(1, far_step, lambda k: ring_step(1, 0, k))
    ring_step(1, 0, far_step, last=True)
    products(1)
    ring_end(1, 0)
    rows_pass(0)

    apply_rows(1)
    ring_start(1, 1)
    send_picks(1, 1, z)
    routed(1, 0)
    forward(1, 0)
    rows_start(1)
    each(1, far_step, lambda k: ring_step(1, 1, k))
    ring_step(1, 1, far_step, last=True)
    ring_end(1, 1)
    rows_pass(1)
    gathered(group_at(0), h_r.at[0])
    gradient_step(0, False)
    gathered(group_at(1), h_r.at[1])
    each(0, BLK, diag_step)
    routed(1, 1)
    forward(1, 1)
    gradient_step(1, True)

    wait_all(score_z.at[pl.ds(1, Z - 1)], exch_s.at[0])
    wait_all(score_y.at[pl.ds(1, Y - 1)], exch_s.at[1])
    wait_all(score_c.at[pl.ds(1, C - 1)], exch_s.at[2])
    gather_sent(window_at, w_s, v_s)
    sent = Z // 2 * BLK - BLK // 2
    for p in range(2):
        for h in range(NC):
            for way in range(2):
                wait_all(field[p][h].at[pl.ds(0, sent)], ring_s.at[p, h, way])
            for i in range(Y - 1):
                wait_all(ysend[p][h].at[pl.ds(i * SLOTS, SLOTS)], y_s.at[p, h, i])
            wait_all(fsend[p][h].at[pl.ds(TD, (C - 1) * TD)], f_s.at[p, h])
    for h in range(NC):
        wait_all(psend[h].at[pl.ds(TD, (C - 1) * TD)], p_s.at[h])
        gather_sent(group_at(h), g_s.at[h], h_s.at[h])
    for t in range(TD):
        pltpu.make_async_copy(tile_f32.at[t], tiles_out.at[t], local.at[1 + t]).wait()


def index_table(tile_rows, tile_cols, row, me):
    y, z = row // Z, row % Z
    tiles = C * TD
    of_group = lambda ids, g: lax.dynamic_slice(ids, (g * tiles,), (tiles,))
    slices = [of_group(tile_cols, ((y + d) % Y) * Z + z) for d in range(Y)]
    *slices, rows = lax.optimization_barrier((*slices, of_group(tile_rows, row)))
    cols = jnp.stack(slices)
    source, local = cols // BLK, cols % BLK
    place = jnp.arange(tiles)
    rank = jnp.sum(
        (source[:, :, None] == source[:, None, :]) & (place[None, :] < place[:, None])[None],
        axis=2,
        dtype=jnp.int32,
    )
    slot = jnp.arange(SLOTS)
    chosen = (source[1:, None, :] == y * Z + slot[None, :, None] // CAP) & (
        rank[1:, None, :] == slot[None, :, None] % CAP
    )
    pick = jnp.sum(jnp.where(chosen, local[1:, None, :], 0), axis=2).reshape(-1)
    plane, depth = source[0] // Z, source[0] % Z
    away = (y - plane + Y) % Y
    fwd = jnp.where(
        away == 0,
        depth * BLK + local[0],
        PLANE + (away - 1) * SLOTS + depth * CAP + rank[0],
    )
    local_rows = rows - row * BLK
    before = (local_rows[None, :] < local_rows[:, None]) | (
        (local_rows[None, :] == local_rows[:, None]) & (place[None, :] < place[:, None])
    )
    position = jnp.sum(before, axis=1, dtype=jnp.int32)
    at = position[None, :] == place[:, None]
    lands = ((place // TD - me + C) % C) * TD + place % TD
    order = jnp.sum(jnp.where(at, lands[None, :], 0), axis=1)
    first = jnp.sum(local_rows[None, :] < local_rows[:, None], axis=1, dtype=jnp.int32)
    same = jnp.sum(jnp.where(at, (position > first)[None, :].astype(jnp.int32), 0), axis=1)
    blocks = jnp.arange(BLK)
    upto = jnp.sum(local_rows[None, :] <= blocks[:, None], axis=1, dtype=jnp.int32)
    count = jnp.sum(local_rows[None, :] == blocks[:, None], axis=1, dtype=jnp.int32)
    mine = (me * TD + jnp.arange(TD))[:, None] == place[None, :]
    my_rows = jnp.sum(jnp.where(mine, local_rows[None, :], 0), axis=1)
    on_diag = jnp.sum(jnp.where(mine, (rows == cols[0])[None, :].astype(jnp.int32), 0), axis=1)
    table = jnp.concatenate(
        [pick, fwd, order, same, jnp.maximum(upto - 1, 0), (count > 0).astype(jnp.int32), on_diag, my_rows]
    )
    return table.astype(jnp.int32)


def per_device(samples, loadings, omega_tiles, omega_diagonal, tile_rows, tile_cols):
    row = lax.axis_index("rows")
    me = lax.axis_index("cols")
    factors = loadings.shape[0]
    ns = NC * SC
    table = index_table(tile_rows, tile_cols, row, me)
    f32 = jnp.float32
    vmem = lambda *shape: pltpu.VMEM(shape, f32)
    dma = lambda *shape: pltpu.SemaphoreType.DMA(shape)
    in_vmem = pl.BlockSpec(memory_space=pltpu.VMEM)
    in_hbm = pl.BlockSpec(memory_space=pltpu.HBM)
    anywhere = pl.BlockSpec(memory_space=pl.ANY)
    n = 2 * NC
    new_tiles, new_diagonal = pl.pallas_call(
        route_kernel,
        out_shape=(
            jax.ShapeDtypeStruct(omega_tiles.shape, f32),
            jax.ShapeDtypeStruct((1, BLK * BS), f32),
        ),
        in_specs=[
            pl.BlockSpec(memory_space=pltpu.SMEM),
            in_hbm,
            in_hbm,
            in_hbm,
            in_hbm,
        ],
        out_specs=(anywhere, in_vmem),
        scratch_shapes=[
            vmem(3, ns, factors),
            vmem(Z, ns, factors),
            vmem(Y, ns, factors),
            vmem(C, ns, factors),
            vmem(C, ns, BLK * BS),
            vmem(BLK, SC, BS),
            vmem(C * TD, SC, BS),
            vmem(ns, BLK * BS),
            pltpu.VMEM(loadings.shape, jnp.bfloat16),
            vmem(1, BLK * BS),
            vmem(TD, BS, BS),
            pltpu.VMEM((TD, BS, BS), jnp.bfloat16),
            pltpu.VMEM((TD, BS, BS), jnp.bfloat16),
        ]
        + [vmem(PLANE + (Y - 1) * SLOTS, SC, BS)] * n
        + [vmem((Y - 1) * SLOTS, SC, BS)] * n
        + [vmem(C * TD, SC, BS)] * n
        + [vmem(TD, C, SC, BS)] * n
        + [vmem(C, BLK, SC, BS)] * n
        + [vmem(C * TD, SC, BS)] * NC
        + [vmem(C * TD, SC, BS)] * NC
        + [
            dma(3),
            dma(3),
            dma(2, NC, 2),
            dma(2, NC, 2, Z // 2 + 1, 2),
            dma(2, NC, Y - 1),
            dma(2, NC, Y - 1),
            dma(2, NC),
            dma(2, NC, TD),
            dma(NC),
            dma(NC),
            dma(NC, C // 2),
            dma(NC, C // 2),
            dma(NC, C // 2),
            dma(NC, C // 2),
            dma(C // 2),
            dma(C // 2),
            dma(C // 2),
            dma(C // 2),
            dma(4 + TD),
        ],
        compiler_params=pltpu.CompilerParams(
            collective_id=0, has_side_effects=True, vmem_limit_bytes=46 * 1024 * 1024
        ),
        name="route",
    )(
        table,
        *(
            pltpu.with_memory_space_constraint(x, pltpu.HBM)
            for x in (samples, loadings, omega_diagonal.reshape(1, BLK * BS), omega_tiles)
        ),
    )

    limit = step_size * penalty
    new_tiles = new_tiles - jnp.clip(new_tiles, -limit, limit)
    return new_tiles, new_diagonal.reshape(-1)


def solution(mesh):
    placed = (
        P("cols", "rows"),
        P(None, "rows"),
        P(("rows", "cols"), None, None),
        P("rows"),
        P(),
        P(),
    )
    return jax.shard_map(
        per_device,
        mesh=mesh,
        in_specs=placed,
        out_specs=(P(("rows", "cols"), None, None), P("rows")),
        check_vma=False,
    )
```

```python
import functools
import jax
import jax.numpy as jnp
from jax import lax
from jax.experimental import pallas as pl
from jax.experimental.pallas import tpu as pltpu
from jax.sharding import PartitionSpec as P

step_size = 0.5
penalty = 0.02
MESH = pl.DeviceIdType.MESH
CAP = 3
Y = 4
Z = 8
C = 8
BLK = 8
TD = 5
NC = 2
SC = 8
BS = 512
PLANE = Z * BLK
SLOTS = Z * CAP

PICK = 0
FWD = PICK + (Y - 1) * SLOTS
ORDER = FWD + C * TD
SAME = ORDER + C * TD
LAST = SAME + C * TD
HAS = LAST + BLK
DIAG = HAS + BLK
ROWS = DIAG + TD
META = ROWS + TD


def split2(x):
    hi = x.astype(jnp.bfloat16)
    return hi, (x - hi.astype(jnp.float32)).astype(jnp.bfloat16)


def split3(x):
    hi, rest = x.astype(jnp.bfloat16), None
    rest = x - hi.astype(jnp.float32)
    mid, low = split2(rest)
    return jnp.concatenate([hi, mid, low], axis=0)


def dot(a, b, dims):
    return lax.dot_general(a, b, (dims, ((), ())), preferred_element_type=jnp.float32)


def wait_all(ref, sem):
    pltpu.make_async_copy(ref, ref, sem).wait()


def route_kernel(
    meta,
    samples_in,
    loadings_in,
    diag_in,
    tiles,
    tiles_out,
    diag_out,
    part,
    score_z,
    score_y,
    score_c,
    window,
    stage,
    seg,
    samples,
    loadings,
    diag,
    tile_f32,
    tile_hi,
    tile_lo,
    *rest,
):
    n = 2 * NC
    pair = lambda flat: (flat[:NC], flat[NC:])
    field, ysend, fsend, frecv, group = (pair(rest[i * n : (i + 1) * n]) for i in range(5))
    rest = rest[5 * n :]
    psend, precv = rest[:NC], rest[NC : 2 * NC]
    (
        exch_s,
        exch_r,
        ring_s,
        ring_r,
        y_s,
        y_r,
        f_s,
        f_r,
        p_s,
        p_r,
        g_s,
        g_r,
        h_s,
        h_r,
        w_s,
        w_r,
        v_s,
        v_r,
        local,
    ) = rest[2 * NC :]

    row = lax.axis_index("rows")
    me = lax.axis_index("cols")
    y, z = row // Z, row % Z
    at_z = lambda d: {"rows": y * Z + (z + d + Z) % Z}
    at_y = lambda d: {"rows": ((y + d) % Y) * Z + z}
    at_c = lambda d: {"cols": (me + d + C) % C}
    side = 1 - 2 * (me % 2)
    other = at_c(side)

    def remote(src, dst, send, recv, where):
        return pltpu.make_async_remote_copy(
            src_ref=src,
            dst_ref=dst,
            send_sem=send,
            recv_sem=recv,
            device_id=where,
            device_id_type=MESH,
        )

    def each(low, high, body):
        lax.fori_loop(low, high, lambda i, _: (body(i), None)[1], None)

    barrier = pltpu.get_barrier_semaphore()

    def greet(where, count):
        each(
            1,
            count,
            lambda d: pl.semaphore_signal(
                barrier, inc=1, device_id=where(d), device_id_type=MESH
            ),
        )

    loads = [
        pltpu.make_async_copy(src, dst, local.at[1 + TD + i])
        for i, (src, dst) in enumerate(
            ((samples_in, samples), (loadings_in, loadings), (diag_in, diag))
        )
    ]
    for load in loads:
        load.start()
    greet(at_z, Z)
    greet(at_y, Y)
    greet(at_c, C)
    tile_copy = pltpu.make_async_copy(tiles, tile_f32, local.at[0])
    tile_copy.start()

    def split_tiles(low, high):
        rows = lax.broadcasted_iota(jnp.int32, (BS // 4, BS), 0)
        cols = lax.broadcasted_iota(jnp.int32, (BS // 4, BS), 1)

        def one(i):
            t, q = i // 4, i % 4
            at = pl.ds(pl.multiple_of(q * (BS // 4), BS // 4), BS // 4)
            flag = jnp.full((BS // 4, BS), meta[DIAG + t], jnp.int32)
            drop = (rows + q * (BS // 4) == cols) & (flag != 0)
            hi, lo = split2(jnp.where(drop, 0.0, tile_f32[t, at]))
            tile_hi[t, at] = hi
            tile_lo[t, at] = lo

        each(low, high, one)

    def score_step(b, total):
        cols = pl.ds(pl.multiple_of(b * BS, BS), BS)
        return total + dot(split3(samples[:, cols]), loadings[:, cols], ((1,), (1,)))

    for load in loads:
        load.wait()
    ns = NC * SC
    total = lax.fori_loop(0, BLK, score_step, jnp.zeros((3 * ns, loadings.shape[0]), jnp.float32))
    part[0] = total[:ns] + total[ns : 2 * ns] + total[2 * ns :]
    pl.semaphore_wait(barrier, Z + Y + C - 3)

    def gather_start(src, place, far_s, far_r, near_s, near_r):
        each(
            1,
            C // 2,
            lambda q: remote(src, place(2 * q), far_s.at[q], far_r.at[q], at_c(2 * q)).start(),
        )
        remote(src, place((side + C) % C), near_s.at[0], near_r.at[0], other).start()

    def gather_pass(place, far_r, near_s, near_r):
        def one(q):
            wait_all(place(2 * q), far_r.at[q])
            remote(
                place(2 * q), place((side + 2 * q + C) % C), near_s.at[q], near_r.at[q], other
            ).start()

        each(1, C // 2, one)

    def gathered(place, near_r):
        each(0, C // 2, lambda q: wait_all(place((2 * q - side + C) % C), near_r.at[q]))

    def gather_sent(place, far_s, near_s):
        each(1, C // 2, lambda q: wait_all(place(2 * q), far_s.at[q]))
        each(0, C // 2, lambda q: wait_all(place(2 * q), near_s.at[q]))

    window_at = lambda d: window.at[d]

    each(
        1,
        Z,
        lambda d: remote(part.at[0], score_z.at[d], exch_s.at[0], exch_r.at[0], at_z(d)).start(),
    )
    gather_start(samples, window_at, w_s, w_r, v_s, v_r)
    wait_all(score_z.at[pl.ds(1, Z - 1)], exch_r.at[0])
    total = part[0]
    for d in range(1, Z):
        total = total + score_z[d]
    part[1] = total
    each(
        1,
        Y,
        lambda d: remote(part.at[1], score_y.at[d], exch_s.at[1], exch_r.at[1], at_y(d)).start(),
    )
    wait_all(score_y.at[pl.ds(1, Y - 1)], exch_r.at[1])
    for d in range(1, Y):
        total = total + score_y[d]
    scores = split3(total)
    part[2] = total

    def residual_step(b):
        cols = pl.ds(pl.multiple_of(b * BS, BS), BS)
        terms = dot(scores, loadings[:, cols], ((1,), (0,)))
        value = samples[:, cols] - (terms[:ns] + terms[ns : 2 * ns] + terms[2 * ns :])
        for h in range(NC):
            field[0][h][z * BLK + b] = value[h * SC : (h + 1) * SC]
            group[0][h][0, b] = value[h * SC : (h + 1) * SC]

    each(0, BLK, residual_step)

    def group_residual():
        gathered(window_at, v_r)
        wait_all(score_c.at[pl.ds(1, C - 1)], exch_r.at[2])
        far = (C - 1) * ns
        terms3 = split3(score_c[1:].reshape(far, loadings.shape[0]))

        def one(b):
            cols = pl.ds(pl.multiple_of(b * BS, BS), BS)
            terms = dot(terms3, loadings[:, cols], ((1,), (0,)))
            terms = terms[:far] + terms[far : 2 * far] + terms[2 * far :]
            value = window[pl.ds(1, C - 1), :, cols] - terms.reshape(C - 1, ns, BS)
            for h in range(NC):
                group[0][h][pl.ds(1, C - 1), b] = value[:, h * SC : (h + 1) * SC]

        each(0, BLK, one)

    half = BLK // 2

    def hop(p, h, k, u, right):
        slice_of = ((z - k + 1 + Z) if right else (z + k - 1)) % Z
        ref = field[p][h].at[pl.ds(slice_of * BLK + u * half, half)]
        way = 0 if right else 1
        return remote(
            ref,
            ref,
            ring_s.at[p, h, way],
            ring_r.at[p, h, way, k, u],
            at_z(1 if right else -1),
        )

    def arrived(p, h, k, u, right):
        slice_of = ((z - k + Z) if right else (z + k)) % Z
        ref = field[p][h].at[pl.ds(slice_of * BLK + u * half, half)]
        wait_all(ref, ring_r.at[p, h, 0 if right else 1, k, u])

    def send_picks(p, h, zs):
        ref = field[p][h]
        stage[...] = ref[pl.ds(zs * BLK, BLK)]

        def to_plane(turn):
            i = (turn + 1) % (Y - 1)
            base = i * SLOTS + zs * CAP
            for j in range(CAP):
                ysend[p][h][base + j] = stage[meta[PICK + base + j]]
            remote(
                ysend[p][h].at[pl.ds(base, CAP)],
                ref.at[pl.ds(PLANE + base, CAP)],
                y_s.at[p, h, i],
                y_r.at[p, h, i],
                at_y(i + 1),
            ).start()

        each(0, Y - 1, to_plane)

    def ring_start(p, h):
        for u in range(2):
            hop(p, h, 1, u, True).start()
            hop(p, h, 1, 1 - u, False).start()

    def ring_step(p, h, k, last=False):
        for u in range(2):
            arrived(p, h, k, u, True)
            if not last or u == 0:
                hop(p, h, k + 1, u, True).start()
            arrived(p, h, k, 1 - u, False)
            if not last or u == 0:
                hop(p, h, k + 1, 1 - u, False).start()
        picks_at(p, h, k)

    def ring_end(p, h):
        arrived(p, h, Z // 2, 0, True)
        arrived(p, h, Z // 2, 1, False)
        send_picks(p, h, (z + Z // 2) % Z)

    def picks_at(p, h, k):
        send_picks(p, h, (z - k + Z) % Z)
        send_picks(p, h, (z + k) % Z)

    def routed(p, h):
        for i in range(Y - 1):
            wait_all(field[p][h].at[pl.ds(PLANE + i * SLOTS, SLOTS)], y_r.at[p, h, i])

    def forward(p, h):
        def tile(t):
            def one(d):
                dest = (me + d) % C
                at = d * TD + t
                fsend[p][h][at] = field[p][h][meta[FWD + dest * TD + t]]
                remote(
                    fsend[p][h].at[at],
                    frecv[p][h].at[t, d],
                    f_s.at[p, h],
                    f_r.at[p, h, t],
                    at_c(d),
                ).start()

            each(1, C, one)
            frecv[p][h][t, 0] = field[p][h][meta[FWD + me * TD + t]]

        each(0, TD, tile)

    def forwarded(p, h, t):
        wait_all(frecv[p][h].at[t, pl.ds(1, C - 1)], f_r.at[p, h, t])

    def products(h):
        def one(t):
            forwarded(0, h, t)
            hi, lo = split2(frecv[0][h][t].reshape(C * SC, BS))
            both = dot(jnp.concatenate([hi, lo], axis=0), tile_hi[t], ((1,), (1,)))
            value = both[: C * SC] + both[C * SC :] + dot(hi, tile_lo[t], ((1,), (1,)))
            value = value.reshape(C, SC, BS)
            precv[h][t] = value[0]
            for d in range(1, C):
                psend[h][d * TD + t] = value[d]
            each(
                1,
                C,
                lambda d: remote(
                    psend[h].at[d * TD + t],
                    precv[h].at[d * TD + t],
                    p_s.at[h],
                    p_r.at[h],
                    at_c(-d),
                ).start(),
            )

        each(0, TD, one)

    def apply_rows(h):
        wait_all(precv[h].at[pl.ds(TD, (C - 1) * TD)], p_r.at[h])

        def one(k, running):
            same = jnp.full((SC, BS), meta[SAME + k], jnp.int32) != 0
            running = jnp.where(same, running, 0.0) + precv[h][meta[ORDER + k]]
            seg[k] = running
            return running

        lax.fori_loop(0, C * TD, one, jnp.zeros((SC, BS), jnp.float32))

        def block(b):
            has = jnp.full((SC, BS), meta[HAS + b], jnp.int32) != 0
            value = jnp.where(has, seg[meta[LAST + b]], 0.0)
            value = value + diag[:, pl.ds(pl.multiple_of(b * BS, BS), BS)] * group[0][h][0, b]
            field[1][h][z * BLK + b] = value
            group[1][h][0, b] = value

        each(0, BLK, block)

    group_at = lambda h: lambda d: group[1][h].at[d]

    def rows_start(h):
        gather_start(group[1][h].at[0], group_at(h), g_s.at[h], g_r.at[h], h_s.at[h], h_r.at[h])

    def rows_pass(h):
        gather_pass(group_at(h), g_r.at[h], h_s.at[h], h_r.at[h])

    scale = step_size * 0.5 / (NC * C * SC)

    def gradient_step(h, finish):
        def one(t):
            forwarded(1, h, t)
            block = meta[ROWS + t]
            rows = lambda p: group[p][h][:, block].reshape(C * SC, BS)
            left_hi, left_lo = split2(jnp.concatenate([rows(1), rows(0)], axis=0))
            right = [frecv[p][h][t].reshape(C * SC, BS) for p in range(2)]
            right_hi, right_lo = split2(jnp.concatenate(right, axis=0))
            left = jnp.concatenate([left_hi, left_hi, left_lo], axis=0)
            right = jnp.concatenate([right_hi, right_lo, right_hi], axis=0)
            total = dot(left, right, ((0,), (0,)))
            stepped = tile_f32[t] - scale * total
            if finish:
                i = lax.broadcasted_iota(jnp.int32, (BS, BS), 0)
                j = lax.broadcasted_iota(jnp.int32, (BS, BS), 1)
                flag = jnp.full((BS, BS), meta[DIAG + t], jnp.int32)
                stepped = jnp.where((i == j) & (flag != 0), 0.0, stepped)
            tile_f32[t] = stepped
            if finish:
                pltpu.make_async_copy(tile_f32.at[t], tiles_out.at[t], local.at[1 + t]).start()

        each(0, TD, one)

    def diag_step(b):
        total = jnp.zeros((SC, BS), jnp.float32)
        for h in range(NC):
            for d in range(C):
                total = total + group[0][h][d, b] * group[1][h][d, b]
        stat = jnp.sum(total, axis=0, keepdims=True) / (NC * C * SC)
        at = pl.ds(pl.multiple_of(b * BS, BS), BS)
        old = diag[:, at]
        diag_out[:, at] = old - step_size * (stat - 1.0 / old)

    far_step = Z // 2 - 1

    ring_start(0, 0)
    send_picks(0, 0, z)
    send_picks(0, 1, z)
    each(
        1,
        C,
        lambda d: remote(part.at[2], score_c.at[d], exch_s.at[2], exch_r.at[2], at_c(d)).start(),
    )
    each(1, far_step, lambda k: ring_step(0, 0, k))
    ring_step(0, 0, far_step, last=True)
    ring_start(0, 1)
    gather_pass(window_at, w_r, v_s, v_r)
    ring_end(0, 0)
    tile_copy.wait()
    split_tiles(0, TD * 4)
    each(1, far_step, lambda k: ring_step(0, 1, k))
    routed(0, 0)
    forward(0, 0)
    ring_step(0, 1, far_step, last=True)
    ring_end(0, 1)
    products(0)
    group_residual()

    routed(0, 1)
    forward(0, 1)
    apply_rows(0)
    ring_start(1, 0)
    send_picks(1, 0, z)
    rows_start(0)
    each(1, far_step, lambda k: ring_step(1, 0, k))
    products(1)
    ring_step(1, 0, far_step, last=True)
    ring_end(1, 0)
    rows_pass(0)

    apply_rows(1)
    ring_start(1, 1)
    send_picks(1, 1, z)
    routed(1, 0)
    forward(1, 0)
    rows_start(1)
    each(1, far_step, lambda k: ring_step(1, 1, k))
    ring_step(1, 1, far_step, last=True)
    ring_end(1, 1)
    rows_pass(1)
    gathered(group_at(0), h_r.at[0])
    gradient_step(0, False)
    gathered(group_at(1), h_r.at[1])
    each(0, BLK, diag_step)
    routed(1, 1)
    forward(1, 1)
    gradient_step(1, True)

    wait_all(score_z.at[pl.ds(1, Z - 1)], exch_s.at[0])
    wait_all(score_y.at[pl.ds(1, Y - 1)], exch_s.at[1])
    wait_all(score_c.at[pl.ds(1, C - 1)], exch_s.at[2])
    gather_sent(window_at, w_s, v_s)
    sent = Z // 2 * BLK - BLK // 2
    for p in range(2):
        for h in range(NC):
            for way in range(2):
                wait_all(field[p][h].at[pl.ds(0, sent)], ring_s.at[p, h, way])
            for i in range(Y - 1):
                wait_all(ysend[p][h].at[pl.ds(i * SLOTS, SLOTS)], y_s.at[p, h, i])
            wait_all(fsend[p][h].at[pl.ds(TD, (C - 1) * TD)], f_s.at[p, h])
    for h in range(NC):
        wait_all(psend[h].at[pl.ds(TD, (C - 1) * TD)], p_s.at[h])
        gather_sent(group_at(h), g_s.at[h], h_s.at[h])
    for t in range(TD):
        pltpu.make_async_copy(tile_f32.at[t], tiles_out.at[t], local.at[1 + t]).wait()


def index_table(tile_rows, tile_cols, row, me):
    y, z = row // Z, row % Z
    tiles = C * TD
    of_group = lambda ids, g: lax.dynamic_slice(ids, (g * tiles,), (tiles,))
    slices = [of_group(tile_cols, ((y + d) % Y) * Z + z) for d in range(Y)]
    ids = lax.optimization_barrier(jnp.stack([*slices, of_group(tile_rows, row)]))
    cols, rows = ids[:Y], ids[Y]
    source, local = cols // BLK, cols % BLK
    place = jnp.arange(tiles)
    rank = jnp.sum(
        (source[:, :, None] == source[:, None, :]) & (place[None, :] < place[:, None])[None],
        axis=2,
        dtype=jnp.int32,
    )
    slot = jnp.arange(SLOTS)
    chosen = (source[1:, None, :] == y * Z + slot[None, :, None] // CAP) & (
        rank[1:, None, :] == slot[None, :, None] % CAP
    )
    pick = jnp.sum(jnp.where(chosen, local[1:, None, :], 0), axis=2).reshape(-1)
    plane, depth = source[0] // Z, source[0] % Z
    away = (y - plane + Y) % Y
    fwd = jnp.where(
        away == 0,
        depth * BLK + local[0],
        PLANE + (away - 1) * SLOTS + depth * CAP + rank[0],
    )
    local_rows = rows - row * BLK
    before = (local_rows[None, :] < local_rows[:, None]) | (
        (local_rows[None, :] == local_rows[:, None]) & (place[None, :] < place[:, None])
    )
    position = jnp.sum(before, axis=1, dtype=jnp.int32)
    at = position[None, :] == place[:, None]
    lands = ((place // TD - me + C) % C) * TD + place % TD
    order = jnp.sum(jnp.where(at, lands[None, :], 0), axis=1)
    first = jnp.sum(local_rows[None, :] < local_rows[:, None], axis=1, dtype=jnp.int32)
    same = jnp.sum(jnp.where(at, (position > first)[None, :].astype(jnp.int32), 0), axis=1)
    blocks = jnp.arange(BLK)
    upto = jnp.sum(local_rows[None, :] <= blocks[:, None], axis=1, dtype=jnp.int32)
    count = jnp.sum(local_rows[None, :] == blocks[:, None], axis=1, dtype=jnp.int32)
    mine = (me * TD + jnp.arange(TD))[:, None] == place[None, :]
    my_rows = jnp.sum(jnp.where(mine, local_rows[None, :], 0), axis=1)
    on_diag = jnp.sum(jnp.where(mine, (rows == cols[0])[None, :].astype(jnp.int32), 0), axis=1)
    table = jnp.concatenate(
        [pick, fwd, order, same, jnp.maximum(upto - 1, 0), (count > 0).astype(jnp.int32), on_diag, my_rows]
    )
    return table.astype(jnp.int32)


def per_device(samples, loadings, omega_tiles, omega_diagonal, tile_rows, tile_cols):
    row = lax.axis_index("rows")
    me = lax.axis_index("cols")
    factors = loadings.shape[0]
    ns = NC * SC
    table = index_table(tile_rows, tile_cols, row, me)
    f32 = jnp.float32
    vmem = lambda *shape: pltpu.VMEM(shape, f32)
    dma = lambda *shape: pltpu.SemaphoreType.DMA(shape)
    in_vmem = pl.BlockSpec(memory_space=pltpu.VMEM)
    in_hbm = pl.BlockSpec(memory_space=pltpu.HBM)
    anywhere = pl.BlockSpec(memory_space=pl.ANY)
    n = 2 * NC
    new_tiles, new_diagonal = pl.pallas_call(
        route_kernel,
        out_shape=(
            jax.ShapeDtypeStruct(omega_tiles.shape, f32),
            jax.ShapeDtypeStruct((1, BLK * BS), f32),
        ),
        in_specs=[
            pl.BlockSpec(memory_space=pltpu.SMEM),
            in_hbm,
            in_hbm,
            in_hbm,
            in_hbm,
        ],
        out_specs=(anywhere, in_vmem),
        scratch_shapes=[
            vmem(3, ns, factors),
            vmem(Z, ns, factors),
            vmem(Y, ns, factors),
            vmem(C, ns, factors),
            vmem(C, ns, BLK * BS),
            vmem(BLK, SC, BS),
            vmem(C * TD, SC, BS),
            vmem(ns, BLK * BS),
            pltpu.VMEM(loadings.shape, jnp.bfloat16),
            vmem(1, BLK * BS),
            vmem(TD, BS, BS),
            pltpu.VMEM((TD, BS, BS), jnp.bfloat16),
            pltpu.VMEM((TD, BS, BS), jnp.bfloat16),
        ]
        + [vmem(PLANE + (Y - 1) * SLOTS, SC, BS)] * n
        + [vmem((Y - 1) * SLOTS, SC, BS)] * n
        + [vmem(C * TD, SC, BS)] * n
        + [vmem(TD, C, SC, BS)] * n
        + [vmem(C, BLK, SC, BS)] * n
        + [vmem(C * TD, SC, BS)] * NC
        + [vmem(C * TD, SC, BS)] * NC
        + [
            dma(3),
            dma(3),
            dma(2, NC, 2),
            dma(2, NC, 2, Z // 2 + 1, 2),
            dma(2, NC, Y - 1),
            dma(2, NC, Y - 1),
            dma(2, NC),
            dma(2, NC, TD),
            dma(NC),
            dma(NC),
            dma(NC, C // 2),
            dma(NC, C // 2),
            dma(NC, C // 2),
            dma(NC, C // 2),
            dma(C // 2),
            dma(C // 2),
            dma(C // 2),
            dma(C // 2),
            dma(4 + TD),
        ],
        compiler_params=pltpu.CompilerParams(
            collective_id=0, has_side_effects=True, vmem_limit_bytes=46 * 1024 * 1024
        ),
        name="route",
    )(
        table,
        *(
            pltpu.with_memory_space_constraint(x, pltpu.HBM)
            for x in (samples, loadings, omega_diagonal.reshape(1, BLK * BS), omega_tiles)
        ),
    )

    limit = step_size * penalty
    new_tiles = new_tiles - jnp.clip(new_tiles, -limit, limit)
    return new_tiles, new_diagonal.reshape(-1)


def solution(mesh):
    placed = (
        P("cols", "rows"),
        P(None, "rows"),
        P(("rows", "cols"), None, None),
        P("rows"),
        P(),
        P(),
    )
    return jax.shard_map(
        per_device,
        mesh=mesh,
        in_specs=placed,
        out_specs=(P(("rows", "cols"), None, None), P("rows")),
        check_vma=False,
    )
```

```python
import functools
import jax
import jax.numpy as jnp
from jax import lax
from jax.experimental import pallas as pl
from jax.experimental.pallas import tpu as pltpu
from jax.sharding import PartitionSpec as P

step_size = 0.5
penalty = 0.02
MESH = pl.DeviceIdType.MESH
CAP = 3
Y = 4
Z = 8
C = 8
BLK = 8
TD = 5
NC = 2
SC = 8
BS = 512
PLANE = Z * BLK
SLOTS = Z * CAP

PICK = 0
FWD = PICK + (Y - 1) * SLOTS
ORDER = FWD + C * TD
SAME = ORDER + C * TD
LAST = SAME + C * TD
HAS = LAST + BLK
DIAG = HAS + BLK
ROWS = DIAG + TD
META = ROWS + TD


def split2(x):
    hi = x.astype(jnp.bfloat16)
    return hi, (x - hi.astype(jnp.float32)).astype(jnp.bfloat16)


def split3(x):
    hi, rest = x.astype(jnp.bfloat16), None
    rest = x - hi.astype(jnp.float32)
    mid, low = split2(rest)
    return jnp.concatenate([hi, mid, low], axis=0)


def dot(a, b, dims):
    return lax.dot_general(a, b, (dims, ((), ())), preferred_element_type=jnp.float32)


def wait_all(ref, sem):
    pltpu.make_async_copy(ref, ref, sem).wait()


def route_kernel(
    meta,
    samples_in,
    loadings_in,
    diag_in,
    tiles,
    tiles_out,
    diag_out,
    part,
    score_z,
    score_y,
    score_c,
    window,
    stage,
    seg,
    samples,
    loadings,
    diag,
    tile_f32,
    tile_hi,
    tile_lo,
    *rest,
):
    n = 2 * NC
    pair = lambda flat: (flat[:NC], flat[NC:])
    field, ysend, fsend, frecv, group = (pair(rest[i * n : (i + 1) * n]) for i in range(5))
    rest = rest[5 * n :]
    psend, precv = rest[:NC], rest[NC : 2 * NC]
    (
        exch_s,
        exch_r,
        ring_s,
        ring_r,
        y_s,
        y_r,
        f_s,
        f_r,
        p_s,
        p_r,
        g_s,
        g_r,
        h_s,
        h_r,
        w_s,
        w_r,
        v_s,
        v_r,
        local,
    ) = rest[2 * NC :]

    row = lax.axis_index("rows")
    me = lax.axis_index("cols")
    y, z = row // Z, row % Z
    at_z = lambda d: {"rows": y * Z + (z + d + Z) % Z}
    at_y = lambda d: {"rows": ((y + d) % Y) * Z + z}
    at_c = lambda d: {"cols": (me + d + C) % C}
    side = 1 - 2 * (me % 2)
    other = at_c(side)

    def remote(src, dst, send, recv, where):
        return pltpu.make_async_remote_copy(
            src_ref=src,
            dst_ref=dst,
            send_sem=send,
            recv_sem=recv,
            device_id=where,
            device_id_type=MESH,
        )

    def each(low, high, body):
        lax.fori_loop(low, high, lambda i, _: (body(i), None)[1], None)

    barrier = pltpu.get_barrier_semaphore()

    def greet(where, count):
        each(
            1,
            count,
            lambda d: pl.semaphore_signal(
                barrier, inc=1, device_id=where(d), device_id_type=MESH
            ),
        )

    loads = [
        pltpu.make_async_copy(src, dst, local.at[1 + TD + i])
        for i, (src, dst) in enumerate(
            ((samples_in, samples), (loadings_in, loadings), (diag_in, diag))
        )
    ]
    for load in loads:
        load.start()
    greet(at_z, Z)
    greet(at_y, Y)
    greet(at_c, C)
    tile_copy = pltpu.make_async_copy(tiles, tile_f32, local.at[0])
    tile_copy.start()

    def split_tiles(low, high):
        rows = lax.broadcasted_iota(jnp.int32, (BS // 4, BS), 0)
        cols = lax.broadcasted_iota(jnp.int32, (BS // 4, BS), 1)

        def one(i):
            t, q = i // 4, i % 4
            at = pl.ds(pl.multiple_of(q * (BS // 4), BS // 4), BS // 4)
            flag = jnp.full((BS // 4, BS), meta[DIAG + t], jnp.int32)
            drop = (rows + q * (BS // 4) == cols) & (flag != 0)
            hi, lo = split2(jnp.where(drop, 0.0, tile_f32[t, at]))
            tile_hi[t, at] = hi
            tile_lo[t, at] = lo

        each(low, high, one)

    def score_step(b, total):
        cols = pl.ds(pl.multiple_of(b * BS, BS), BS)
        return total + dot(split3(samples[:, cols]), loadings[:, cols], ((1,), (1,)))

    for load in loads:
        load.wait()
    ns = NC * SC
    total = lax.fori_loop(0, BLK, score_step, jnp.zeros((3 * ns, loadings.shape[0]), jnp.float32))
    part[0] = total[:ns] + total[ns : 2 * ns] + total[2 * ns :]
    pl.semaphore_wait(barrier, Z + Y + C - 3)

    def gather_start(src, place, far_s, far_r, near_s, near_r):
        each(
            1,
            C // 2,
            lambda q: remote(src, place(2 * q), far_s.at[q], far_r.at[q], at_c(2 * q)).start(),
        )
        remote(src, place((side + C) % C), near_s.at[0], near_r.at[0], other).start()

    def gather_pass(place, far_r, near_s, near_r):
        def one(q):
            wait_all(place(2 * q), far_r.at[q])
            remote(
                place(2 * q), place((side + 2 * q + C) % C), near_s.at[q], near_r.at[q], other
            ).start()

        each(1, C // 2, one)

    def gathered(place, near_r):
        each(0, C // 2, lambda q: wait_all(place((2 * q - side + C) % C), near_r.at[q]))

    def gather_sent(place, far_s, near_s):
        each(1, C // 2, lambda q: wait_all(place(2 * q), far_s.at[q]))
        each(0, C // 2, lambda q: wait_all(place(2 * q), near_s.at[q]))

    window_at = lambda d: window.at[d]

    each(
        1,
        Z,
        lambda d: remote(part.at[0], score_z.at[d], exch_s.at[0], exch_r.at[0], at_z(d)).start(),
    )
    gather_start(samples, window_at, w_s, w_r, v_s, v_r)
    wait_all(score_z.at[pl.ds(1, Z - 1)], exch_r.at[0])
    total = part[0]
    for d in range(1, Z):
        total = total + score_z[d]
    part[1] = total
    each(
        1,
        Y,
        lambda d: remote(part.at[1], score_y.at[d], exch_s.at[1], exch_r.at[1], at_y(d)).start(),
    )
    wait_all(score_y.at[pl.ds(1, Y - 1)], exch_r.at[1])
    for d in range(1, Y):
        total = total + score_y[d]
    scores = split3(total)
    part[2] = total

    def residual_step(b):
        cols = pl.ds(pl.multiple_of(b * BS, BS), BS)
        terms = dot(scores, loadings[:, cols], ((1,), (0,)))
        value = samples[:, cols] - (terms[:ns] + terms[ns : 2 * ns] + terms[2 * ns :])
        for h in range(NC):
            field[0][h][z * BLK + b] = value[h * SC : (h + 1) * SC]
            group[0][h][0, b] = value[h * SC : (h + 1) * SC]

    each(0, BLK, residual_step)

    def group_residual():
        gathered(window_at, v_r)
        wait_all(score_c.at[pl.ds(1, C - 1)], exch_r.at[2])
        far = (C - 1) * ns
        terms3 = split3(score_c[1:].reshape(far, loadings.shape[0]))

        def one(b):
            cols = pl.ds(pl.multiple_of(b * BS, BS), BS)
            terms = dot(terms3, loadings[:, cols], ((1,), (0,)))
            terms = terms[:far] + terms[far : 2 * far] + terms[2 * far :]
            value = window[pl.ds(1, C - 1), :, cols] - terms.reshape(C - 1, ns, BS)
            for h in range(NC):
                group[0][h][pl.ds(1, C - 1), b] = value[:, h * SC : (h + 1) * SC]

        each(0, BLK, one)

    half = BLK // 2

    def hop(p, h, k, u, right):
        slice_of = ((z - k + 1 + Z) if right else (z + k - 1)) % Z
        ref = field[p][h].at[pl.ds(slice_of * BLK + u * half, half)]
        way = 0 if right else 1
        return remote(
            ref,
            ref,
            ring_s.at[p, h, way],
            ring_r.at[p, h, way, k, u],
            at_z(1 if right else -1),
        )

    def arrived(p, h, k, u, right):
        slice_of = ((z - k + Z) if right else (z + k)) % Z
        ref = field[p][h].at[pl.ds(slice_of * BLK + u * half, half)]
        wait_all(ref, ring_r.at[p, h, 0 if right else 1, k, u])

    def send_picks(p, h, zs):
        ref = field[p][h]
        stage[...] = ref[pl.ds(zs * BLK, BLK)]

        def to_plane(turn):
            i = (turn + 1) % (Y - 1)
            base = i * SLOTS + zs * CAP
            for j in range(CAP):
                ysend[p][h][base + j] = stage[meta[PICK + base + j]]
            remote(
                ysend[p][h].at[pl.ds(base, CAP)],
                ref.at[pl.ds(PLANE + base, CAP)],
                y_s.at[p, h, i],
                y_r.at[p, h, i],
                at_y(i + 1),
            ).start()

        each(0, Y - 1, to_plane)

    def ring_start(p, h):
        for u in range(2):
            hop(p, h, 1, u, True).start()
            hop(p, h, 1, 1 - u, False).start()

    def ring_step(p, h, k, last=False):
        for u in range(2):
            arrived(p, h, k, u, True)
            if not last or u == 0:
                hop(p, h, k + 1, u, True).start()
            arrived(p, h, k, 1 - u, False)
            if not last or u == 0:
                hop(p, h, k + 1, 1 - u, False).start()
        picks_at(p, h, k)

    def ring_end(p, h):
        arrived(p, h, Z // 2, 0, True)
        arrived(p, h, Z // 2, 1, False)
        send_picks(p, h, (z + Z // 2) % Z)

    def picks_at(p, h, k):
        send_picks(p, h, (z - k + Z) % Z)
        send_picks(p, h, (z + k) % Z)

    def routed(p, h):
        for i in range(Y - 1):
            wait_all(field[p][h].at[pl.ds(PLANE + i * SLOTS, SLOTS)], y_r.at[p, h, i])

    def forward(p, h):
        def tile(t):
            def one(d):
                dest = (me + d) % C
                at = d * TD + t
                fsend[p][h][at] = field[p][h][meta[FWD + dest * TD + t]]
                remote(
                    fsend[p][h].at[at],
                    frecv[p][h].at[t, d],
                    f_s.at[p, h],
                    f_r.at[p, h, t],
                    at_c(d),
                ).start()

            each(1, C, one)
            frecv[p][h][t, 0] = field[p][h][meta[FWD + me * TD + t]]

        each(0, TD, tile)

    def forwarded(p, h, t):
        wait_all(frecv[p][h].at[t, pl.ds(1, C - 1)], f_r.at[p, h, t])

    def products(h):
        def one(t):
            forwarded(0, h, t)
            hi, lo = split2(frecv[0][h][t].reshape(C * SC, BS))
            both = dot(jnp.concatenate([hi, lo], axis=0), tile_hi[t], ((1,), (1,)))
            value = both[: C * SC] + both[C * SC :] + dot(hi, tile_lo[t], ((1,), (1,)))
            value = value.reshape(C, SC, BS)
            precv[h][t] = value[0]
            for d in range(1, C):
                psend[h][d * TD + t] = value[d]
            each(
                1,
                C,
                lambda d: remote(
                    psend[h].at[d * TD + t],
                    precv[h].at[d * TD + t],
                    p_s.at[h],
                    p_r.at[h],
                    at_c(-d),
                ).start(),
            )

        each(0, TD, one)

    def apply_rows(h):
        wait_all(precv[h].at[pl.ds(TD, (C - 1) * TD)], p_r.at[h])

        def one(k, running):
            same = jnp.full((SC, BS), meta[SAME + k], jnp.int32) != 0
            running = jnp.where(same, running, 0.0) + precv[h][meta[ORDER + k]]
            seg[k] = running
            return running

        lax.fori_loop(0, C * TD, one, jnp.zeros((SC, BS), jnp.float32))

        def block(b):
            has = jnp.full((SC, BS), meta[HAS + b], jnp.int32) != 0
            value = jnp.where(has, seg[meta[LAST + b]], 0.0)
            value = value + diag[:, pl.ds(pl.multiple_of(b * BS, BS), BS)] * group[0][h][0, b]
            field[1][h][z * BLK + b] = value
            group[1][h][0, b] = value

        each(0, BLK, block)

    group_at = lambda h: lambda d: group[1][h].at[d]

    def rows_start(h):
        gather_start(group[1][h].at[0], group_at(h), g_s.at[h], g_r.at[h], h_s.at[h], h_r.at[h])

    def rows_pass(h):
        gather_pass(group_at(h), g_r.at[h], h_s.at[h], h_r.at[h])

    scale = step_size * 0.5 / (NC * C * SC)

    def gradient_step(h, finish):
        def one(t):
            forwarded(1, h, t)
            block = meta[ROWS + t]
            rows = lambda p: group[p][h][:, block].reshape(C * SC, BS)
            left_hi, left_lo = split2(jnp.concatenate([rows(1), rows(0)], axis=0))
            right = [frecv[p][h][t].reshape(C * SC, BS) for p in range(2)]
            right_hi, right_lo = split2(jnp.concatenate(right, axis=0))
            left = jnp.concatenate([left_hi, left_hi, left_lo], axis=0)
            right = jnp.concatenate([right_hi, right_lo, right_hi], axis=0)
            total = dot(left, right, ((0,), (0,)))
            stepped = tile_f32[t] - scale * total
            if finish:
                i = lax.broadcasted_iota(jnp.int32, (BS, BS), 0)
                j = lax.broadcasted_iota(jnp.int32, (BS, BS), 1)
                flag = jnp.full((BS, BS), meta[DIAG + t], jnp.int32)
                stepped = jnp.where((i == j) & (flag != 0), 0.0, stepped)
            tile_f32[t] = stepped
            if finish:
                pltpu.make_async_copy(tile_f32.at[t], tiles_out.at[t], local.at[1 + t]).start()

        each(0, TD, one)

    def diag_step(b):
        total = jnp.zeros((SC, BS), jnp.float32)
        for h in range(NC):
            for d in range(C):
                total = total + group[0][h][d, b] * group[1][h][d, b]
        stat = jnp.sum(total, axis=0, keepdims=True) / (NC * C * SC)
        at = pl.ds(pl.multiple_of(b * BS, BS), BS)
        old = diag[:, at]
        diag_out[:, at] = old - step_size * (stat - 1.0 / old)

    far_step = Z // 2 - 1

    ring_start(0, 0)
    send_picks(0, 0, z)
    send_picks(0, 1, z)
    each(
        1,
        C,
        lambda d: remote(part.at[2], score_c.at[d], exch_s.at[2], exch_r.at[2], at_c(d)).start(),
    )
    each(1, far_step, lambda k: ring_step(0, 0, k))
    ring_step(0, 0, far_step, last=True)
    ring_start(0, 1)
    gather_pass(window_at, w_r, v_s, v_r)
    ring_end(0, 0)
    tile_copy.wait()
    split_tiles(0, TD * 4)
    each(1, far_step, lambda k: ring_step(0, 1, k))
    routed(0, 0)
    forward(0, 0)
    ring_step(0, 1, far_step, last=True)
    ring_end(0, 1)
    products(0)
    group_residual()

    routed(0, 1)
    forward(0, 1)
    apply_rows(0)
    ring_start(1, 0)
    send_picks(1, 0, z)
    rows_start(0)
    ring_step(1, 0, 1)
    products(1)
    each(2, far_step, lambda k: ring_step(1, 0, k))
    ring_step(1, 0, far_step, last=True)
    ring_end(1, 0)
    rows_pass(0)

    apply_rows(1)
    ring_start(1, 1)
    send_picks(1, 1, z)
    routed(1, 0)
    forward(1, 0)
    rows_start(1)
    each(1, far_step, lambda k: ring_step(1, 1, k))
    ring_step(1, 1, far_step, last=True)
    ring_end(1, 1)
    rows_pass(1)
    gathered(group_at(0), h_r.at[0])
    gradient_step(0, False)
    gathered(group_at(1), h_r.at[1])
    each(0, BLK, diag_step)
    routed(1, 1)
    forward(1, 1)
    gradient_step(1, True)

    wait_all(score_z.at[pl.ds(1, Z - 1)], exch_s.at[0])
    wait_all(score_y.at[pl.ds(1, Y - 1)], exch_s.at[1])
    wait_all(score_c.at[pl.ds(1, C - 1)], exch_s.at[2])
    gather_sent(window_at, w_s, v_s)
    sent = Z // 2 * BLK - BLK // 2
    for p in range(2):
        for h in range(NC):
            for way in range(2):
                wait_all(field[p][h].at[pl.ds(0, sent)], ring_s.at[p, h, way])
            for i in range(Y - 1):
                wait_all(ysend[p][h].at[pl.ds(i * SLOTS, SLOTS)], y_s.at[p, h, i])
            wait_all(fsend[p][h].at[pl.ds(TD, (C - 1) * TD)], f_s.at[p, h])
    for h in range(NC):
        wait_all(psend[h].at[pl.ds(TD, (C - 1) * TD)], p_s.at[h])
        gather_sent(group_at(h), g_s.at[h], h_s.at[h])
    for t in range(TD):
        pltpu.make_async_copy(tile_f32.at[t], tiles_out.at[t], local.at[1 + t]).wait()


def index_table(tile_rows, tile_cols, row, me):
    y, z = row // Z, row % Z
    tiles = C * TD
    of_group = lambda ids, g: lax.dynamic_slice(ids, (g * tiles,), (tiles,))
    slices = [of_group(tile_cols, ((y + d) % Y) * Z + z) for d in range(Y)]
    ids = lax.optimization_barrier(jnp.stack([*slices, of_group(tile_rows, row)]))
    cols, rows = ids[:Y], ids[Y]
    source, local = cols // BLK, cols % BLK
    place = jnp.arange(tiles)
    rank = jnp.sum(
        (source[:, :, None] == source[:, None, :]) & (place[None, :] < place[:, None])[None],
        axis=2,
        dtype=jnp.int32,
    )
    slot = jnp.arange(SLOTS)
    chosen = (source[1:, None, :] == y * Z + slot[None, :, None] // CAP) & (
        rank[1:, None, :] == slot[None, :, None] % CAP
    )
    pick = jnp.sum(jnp.where(chosen, local[1:, None, :], 0), axis=2).reshape(-1)
    plane, depth = source[0] // Z, source[0] % Z
    away = (y - plane + Y) % Y
    fwd = jnp.where(
        away == 0,
        depth * BLK + local[0],
        PLANE + (away - 1) * SLOTS + depth * CAP + rank[0],
    )
    local_rows = rows - row * BLK
    before = (local_rows[None, :] < local_rows[:, None]) | (
        (local_rows[None, :] == local_rows[:, None]) & (place[None, :] < place[:, None])
    )
    position = jnp.sum(before, axis=1, dtype=jnp.int32)
    at = position[None, :] == place[:, None]
    lands = ((place // TD - me + C) % C) * TD + place % TD
    order = jnp.sum(jnp.where(at, lands[None, :], 0), axis=1)
    first = jnp.sum(local_rows[None, :] < local_rows[:, None], axis=1, dtype=jnp.int32)
    same = jnp.sum(jnp.where(at, (position > first)[None, :].astype(jnp.int32), 0), axis=1)
    blocks = jnp.arange(BLK)
    upto = jnp.sum(local_rows[None, :] <= blocks[:, None], axis=1, dtype=jnp.int32)
    count = jnp.sum(local_rows[None, :] == blocks[:, None], axis=1, dtype=jnp.int32)
    mine = (me * TD + jnp.arange(TD))[:, None] == place[None, :]
    my_rows = jnp.sum(jnp.where(mine, local_rows[None, :], 0), axis=1)
    on_diag = jnp.sum(jnp.where(mine, (rows == cols[0])[None, :].astype(jnp.int32), 0), axis=1)
    table = jnp.concatenate(
        [pick, fwd, order, same, jnp.maximum(upto - 1, 0), (count > 0).astype(jnp.int32), on_diag, my_rows]
    )
    return table.astype(jnp.int32)


def per_device(samples, loadings, omega_tiles, omega_diagonal, tile_rows, tile_cols):
    row = lax.axis_index("rows")
    me = lax.axis_index("cols")
    factors = loadings.shape[0]
    ns = NC * SC
    table = index_table(tile_rows, tile_cols, row, me)
    f32 = jnp.float32
    vmem = lambda *shape: pltpu.VMEM(shape, f32)
    dma = lambda *shape: pltpu.SemaphoreType.DMA(shape)
    in_vmem = pl.BlockSpec(memory_space=pltpu.VMEM)
    in_hbm = pl.BlockSpec(memory_space=pltpu.HBM)
    anywhere = pl.BlockSpec(memory_space=pl.ANY)
    n = 2 * NC
    new_tiles, new_diagonal = pl.pallas_call(
        route_kernel,
        out_shape=(
            jax.ShapeDtypeStruct(omega_tiles.shape, f32),
            jax.ShapeDtypeStruct((1, BLK * BS), f32),
        ),
        in_specs=[
            pl.BlockSpec(memory_space=pltpu.SMEM),
            in_hbm,
            in_hbm,
            in_hbm,
            in_hbm,
        ],
        out_specs=(anywhere, in_vmem),
        scratch_shapes=[
            vmem(3, ns, factors),
            vmem(Z, ns, factors),
            vmem(Y, ns, factors),
            vmem(C, ns, factors),
            vmem(C, ns, BLK * BS),
            vmem(BLK, SC, BS),
            vmem(C * TD, SC, BS),
            vmem(ns, BLK * BS),
            pltpu.VMEM(loadings.shape, jnp.bfloat16),
            vmem(1, BLK * BS),
            vmem(TD, BS, BS),
            pltpu.VMEM((TD, BS, BS), jnp.bfloat16),
            pltpu.VMEM((TD, BS, BS), jnp.bfloat16),
        ]
        + [vmem(PLANE + (Y - 1) * SLOTS, SC, BS)] * n
        + [vmem((Y - 1) * SLOTS, SC, BS)] * n
        + [vmem(C * TD, SC, BS)] * n
        + [vmem(TD, C, SC, BS)] * n
        + [vmem(C, BLK, SC, BS)] * n
        + [vmem(C * TD, SC, BS)] * NC
        + [vmem(C * TD, SC, BS)] * NC
        + [
            dma(3),
            dma(3),
            dma(2, NC, 2),
            dma(2, NC, 2, Z // 2 + 1, 2),
            dma(2, NC, Y - 1),
            dma(2, NC, Y - 1),
            dma(2, NC),
            dma(2, NC, TD),
            dma(NC),
            dma(NC),
            dma(NC, C // 2),
            dma(NC, C // 2),
            dma(NC, C // 2),
            dma(NC, C // 2),
            dma(C // 2),
            dma(C // 2),
            dma(C // 2),
            dma(C // 2),
            dma(4 + TD),
        ],
        compiler_params=pltpu.CompilerParams(
            collective_id=0, has_side_effects=True, vmem_limit_bytes=46 * 1024 * 1024
        ),
        name="route",
    )(
        table,
        *(
            pltpu.with_memory_space_constraint(x, pltpu.HBM)
            for x in (samples, loadings, omega_diagonal.reshape(1, BLK * BS), omega_tiles)
        ),
    )

    limit = step_size * penalty
    new_tiles = new_tiles - jnp.clip(new_tiles, -limit, limit)
    return new_tiles, new_diagonal.reshape(-1)


def solution(mesh):
    placed = (
        P("cols", "rows"),
        P(None, "rows"),
        P(("rows", "cols"), None, None),
        P("rows"),
        P(),
        P(),
    )
    return jax.shard_map(
        per_device,
        mesh=mesh,
        in_specs=placed,
        out_specs=(P(("rows", "cols"), None, None), P("rows")),
        check_vma=False,
    )
```
